128 devices in a mesh: section: 2 (over x_lo), dp: 32 (over x_hi, y, z), tensor: 2 (over core).
Axes of the slice: x: 4 (x_hi: 2, x_lo: 2; x = x_hi * 2 + x_lo), y: 4, z: 4, core: 2. Of those that a mesh axis runs over, the one named last changes fastest.
Arguments:
- inputs: bfloat16 [2, 4096, 1024], P(None, ('dp', 'tensor')), may hold values from -6 to 6
- cotangent: bfloat16 [2, 4096, 1024], P(None, ('dp', 'tensor')), may hold values from -6 to 6
- segments: int32 [2, 4096], replicated, may hold values from 0 to 23, as said below
- qkv_weight: bfloat16 [2, 3, 1024, 1024], P('section', None, 'dp', 'tensor'), may hold values from -0.1875 to 0.1875
- out_weight: bfloat16 [2, 1024, 1024], P('section', 'tensor', 'dp'), may hold values from -3 to 3
- up_weight: bfloat16 [2, 1024, 4096], P('section', 'dp', 'tensor'), may hold values from -0.1875 to 0.1875
- down_weight: bfloat16 [2, 4096, 1024], P('section', 'tensor', 'dp'), may hold values from -0.09375 to 0.09375
- norm_gains: bfloat16 [2, 2, 1024], P('section'), may hold values from 0.5 to 1.5
- biases: bfloat16 [2, 4, 1024], P('section'), may hold values from -2 to 2
- qv_bias: bfloat16 [2, 2, 32, 32], P('section', None, 'tensor', 'dp'), may hold values from -2 to 2
- up_bias: bfloat16 [2, 128, 32], P('section', 'tensor', 'dp'), may hold values from -2 to 2
Outputs:
- activations: bfloat16 [2, 2, 4096, 1024], P('section', None, ('dp', 'tensor'))
- input_grads: bfloat16 [2, 2, 4096, 1024], P('section', None, ('dp', 'tensor'))
- grad_qkv: float32 [2, 3, 1024, 1024], P('section', None, 'dp', 'tensor')
- grad_out: float32 [2, 1024, 1024], P('section', 'tensor', 'dp')
- grad_up: float32 [2, 1024, 4096], P('section', 'dp', 'tensor')
- grad_down: float32 [2, 4096, 1024], P('section', 'tensor', 'dp')
- grad_gains: float32 [2, 2, 1024], P('section')
- grad_biases: float32 [2, 4, 1024], P('section')
- grad_qv_bias: float32 [2, 2, 32, 32], P('section', None, 'tensor', 'dp')
- grad_up_bias: float32 [2, 128, 32], P('section', 'tensor', 'dp')
The draws below stay inside these ranges and needn't reach their ends.
Inputs may be any that keep to these rules, and one draw needn't show every extreme that they name: `segments`: each micro-batch is one packed sequence made of aligned runs of 512 tokens; run i holds three documents numbered 3 i, 3 i + 1 and 3 i + 2 in order, the middle one exactly 400 tokens, the others 30 tokens or more.
All inputs are finite; a program needn't handle non-finite values.
Results may differ from the reference program's by a relative error of at most 0.033.
Values may be sent and summed in bfloat16 or wider, within the bound.
No kernel may reach another device: no remote copies, remote signals or barrier semaphores. Data moves between devices by JAX's collectives and lax.ppermute only.
A program may use at most 128 MiB of HBM per device.

```python
import jax
import jax.numpy as jnp
from jax import lax

D = 1024
HEADS = 16
FF = 4096
HD = 64
MICRO = 2
VEC = 32
SEQ_LEN = 512
SEQ = 4096
DOC_MOST = 400
MIN_DOC = 30
N_SECTION = 2


def draw_segments(key, part):
    key = jax.random.fold_in(key, 11)
    count = SEQ // SEQ_LEN
    starts = jax.random.randint(key, (MICRO, count, 1), MIN_DOC, SEQ_LEN - DOC_MOST - MIN_DOC + 1)
    offsets = jnp.arange(SEQ_LEN, dtype=jnp.int32)[None, None, :]
    inner = (offsets >= starts).astype(jnp.int32) + (offsets >= starts + DOC_MOST).astype(jnp.int32)
    number = 3 * jnp.arange(count, dtype=jnp.int32)[None, :, None] + inner
    return number.reshape(MICRO, SEQ).astype(jnp.int32)


def levels(own_key, dims, cuts, least, largest):
    level, own = 1.0, jax.random.fold_in(own_key, 6)
    for dim, blocks in cuts:
        steps = jnp.exp(jax.random.uniform(jax.random.fold_in(own, dim), (blocks,), jnp.float32, least / len(cuts), largest / len(cuts)))
        level = level * jnp.repeat(steps, dims[dim] // blocks).reshape([-1 if axis == dim else 1 for axis in range(len(dims))])
    return level


def bell_draw(rng, dims, scale, limit, split=(), held_as=jnp.bfloat16):
    result = scale * jax.random.normal(rng, dims, jnp.float32)
    if split:
        result = result * levels(rng, dims, split, -0.22, 0.18)
    return jnp.clip(result, -limit, limit).astype(held_as)


def setup_inputs(seed: int = 0) -> dict:
    streams_of = jax.random.split(jax.random.key(seed), 12)
    return {
        "inputs": bell_draw(streams_of[0], (MICRO, SEQ, D), 1.0, 6.0, ((1, 64),)),
        "cotangent": bell_draw(streams_of[1], (MICRO, SEQ, D), 1.0, 6.0, ((1, 64),)),
        "segments": draw_segments(jax.random.fold_in(streams_of[11], 71), 0),
        "qkv_weight": bell_draw(streams_of[3], (N_SECTION, 3, D, D), D ** -0.5, 0.1875, ((0, 2), (2, 32), (3, 2))),
        "out_weight": bell_draw(streams_of[4], (N_SECTION, D, D), (max(1, D // 256)) ** -0.5, 3.0, ((0, 2), (1, 2), (2, 32))),
        "up_weight": bell_draw(streams_of[5], (N_SECTION, D, FF), D ** -0.5, 0.1875, ((0, 2), (1, 32), (2, 2))),
        "down_weight": bell_draw(streams_of[6], (N_SECTION, FF, D), FF ** -0.5, 0.09375, ((0, 2), (1, 2), (2, 32))),
        "norm_gains": jnp.clip(1.0 + 0.1 * jax.random.normal(streams_of[7], (N_SECTION, 2, D), jnp.float32), 0.5, 1.5).astype(jnp.bfloat16),
        "biases": bell_draw(streams_of[8], (N_SECTION, 4, D), 0.3, 2.0, ((0, 2),)),
        "qv_bias": bell_draw(streams_of[9], (N_SECTION, 2, D // VEC, VEC), 0.3, 2.0, ((0, 2), (2, 2), (3, 32))),
        "up_bias": bell_draw(streams_of[10], (N_SECTION, FF // VEC, VEC), 0.3, 2.0, ((0, 2), (1, 2), (2, 32))),
    }


NORM_EPSILON = 1e-05
MASKED_SCORE = -1e+30

@jax.custom_vjp
def low(v):
    return lax.optimization_barrier(v.astype(jnp.bfloat16)).astype(jnp.float32)

@jax.custom_vjp
def low_back(v):
    return v

def low_keep(v):
    return (low(v), None)

def low_pass(kept, grad):
    return (grad,)

def back_keep(v):
    return (v, None)

def back_low(kept, grad):
    return (low(grad),)
low.defvjp(low_keep, low_pass)
low_back.defvjp(back_keep, back_low)

def norm_rows(values, gain, shift):
    centred = values - lax.optimization_barrier(jnp.mean(values, axis=-1, keepdims=True))
    spread = lax.optimization_barrier(jnp.mean(centred * centred, axis=-1, keepdims=True))
    return centred * lax.rsqrt(spread + NORM_EPSILON) * gain + shift

def matmul_high(left, right):
    return jnp.dot(left, right, precision=lax.Precision.HIGHEST)

def attend(query, keys, values, segment_row):
    length = query.shape[0]
    block_size = min(512, length)
    block_count = length // block_size
    scale = HD ** (-0.5)
    positions = jnp.arange(length, dtype=jnp.int32)
    key_heads = keys.reshape(length, HEADS, HD)
    value_heads = values.reshape(length, HEADS, HD)

    def one_block(pieces):
        query_block, query_pos, query_seg = pieces
        scores = jnp.einsum('qhd,khd->hqk', query_block, key_heads, precision=lax.Precision.HIGHEST) * scale
        scores = low_back(scores)
        allowed = (positions[None, :] <= query_pos[:, None]) & (segment_row[None, :] == query_seg[:, None])
        scores = jnp.where(allowed[None], scores, MASKED_SCORE)
        row_max = lax.optimization_barrier(jnp.max(scores, axis=-1, keepdims=True))
        weights_exp = jnp.where(allowed[None], jnp.exp(scores - row_max), 0.0)
        row_total = lax.optimization_barrier(jnp.sum(weights_exp, axis=-1))
        mixed = jnp.einsum('hqk,khd->qhd', low(weights_exp), value_heads, precision=lax.Precision.HIGHEST)
        return mixed / jnp.transpose(row_total)[:, :, None]
    outputs = lax.map(jax.checkpoint(one_block), (query.reshape(block_count, block_size, HEADS, HD), positions.reshape(block_count, block_size), segment_row.reshape(block_count, block_size)))
    return outputs.reshape(length, HEADS * HD)

def layer_forward(hidden_in, qkv_matrix, out_matrix, up_matrix, down_matrix, gain_rows, shift_rows, qv_rows, up_shift, segment_row):
    normed = low(norm_rows(hidden_in, gain_rows[0], shift_rows[0]))
    query = low_back(low(matmul_high(normed, qkv_matrix[0]) + qv_rows[0]))
    keys = low_back(low(matmul_high(normed, qkv_matrix[1])))
    values = low_back(low(matmul_high(normed, qkv_matrix[2]) + qv_rows[1]))
    attended = low_back(low(attend(query, keys, values, segment_row)))
    hidden = hidden_in + low_back(matmul_high(attended, out_matrix) + shift_rows[2])
    second = low(norm_rows(hidden, gain_rows[1], shift_rows[1]))
    up_pre = low_back(matmul_high(second, up_matrix) + up_shift)
    gelu_low = low(jax.nn.gelu(up_pre, approximate=True))
    return hidden + low_back(matmul_high(gelu_low, down_matrix) + shift_rows[3])

def reference(inputs, cotangent, segments, qkv_weight, out_weight, up_weight, down_weight, norm_gains, biases, qv_bias, up_bias):

    def section_params(level):
        return (qkv_weight[level].astype(jnp.float32), out_weight[level].astype(jnp.float32), up_weight[level].astype(jnp.float32), down_weight[level].astype(jnp.float32), norm_gains[level].astype(jnp.float32), biases[level].astype(jnp.float32), qv_bias[level].astype(jnp.float32).reshape(2, D), up_bias[level].astype(jnp.float32).reshape(FF))
    params_first = section_params(0)
    params_second = section_params(1)
    totals_first = None
    totals_second = None
    outs_first = []
    outs_second = []
    grads_first = []
    grads_second = []
    for micro_index in range(MICRO):
        segment_row = segments[micro_index]

        def apply_layer(hidden_in, *params):
            return layer_forward(hidden_in, *params, segment_row)
        section_input = inputs[micro_index].astype(jnp.float32)
        middle, back_first = jax.vjp(apply_layer, section_input, *params_first)
        middle_low = middle.astype(jnp.bfloat16)
        final_rows, back_second = jax.vjp(apply_layer, middle_low.astype(jnp.float32), *params_second)
        second_grads = back_second(cotangent[micro_index].astype(jnp.float32))
        middle_grad = second_grads[0].astype(jnp.bfloat16)
        first_grads = back_first(middle_grad.astype(jnp.float32))
        outs_first.append(middle_low)
        outs_second.append(final_rows.astype(jnp.bfloat16))
        grads_first.append(first_grads[0].astype(jnp.bfloat16))
        grads_second.append(middle_grad)
        if totals_first is None:
            totals_first = first_grads[1:]
            totals_second = second_grads[1:]
        else:
            totals_first = tuple((left + right for left, right in zip(totals_first, first_grads[1:])))
            totals_second = tuple((left + right for left, right in zip(totals_second, second_grads[1:])))
    activations = jnp.stack([jnp.stack(outs_first), jnp.stack(outs_second)])
    input_grads = jnp.stack([jnp.stack(grads_first), jnp.stack(grads_second)])
    stacked = [jnp.stack([left, right]).astype(jnp.float32) for left, right in zip(totals_first, totals_second)]
    grad_qv_bias = stacked[6].reshape(2, 2, D // VEC, VEC)
    grad_up_bias = stacked[7].reshape(2, FF // VEC, VEC)
    return (activations, input_grads, stacked[0], stacked[1], stacked[2], stacked[3], stacked[4], stacked[5], grad_qv_bias, grad_up_bias)
```

```python
import jax
import jax.numpy as jnp
from jax import lax
from jax.experimental import pallas as pl
from jax.experimental.pallas import tpu as pltpu
from jax.sharding import Mesh, PartitionSpec as P

D = 1024
HD = 64
VEC = 32
RUN = 512
EPS = 1e-05
MASKED = -1e30
BF = jnp.bfloat16
F32 = jnp.float32
ATT = 512
SIDE = 128
MLP = 1024
MIB = 1024 * 1024


def call(body, outs, *args, flops=0, bytes_accessed=2 * MIB, scalars=0, vmem=40):
    specs = [pl.BlockSpec(memory_space=pltpu.SMEM)] * scalars
    specs += [pl.BlockSpec(memory_space=pltpu.VMEM)] * (len(args) - scalars)
    return pl.pallas_call(
        body,
        out_shape=[jax.ShapeDtypeStruct(shape, dtype) for shape, dtype in outs],
        in_specs=specs,
        out_specs=[pl.BlockSpec(memory_space=pltpu.VMEM)] * len(outs),
        compiler_params=pltpu.CompilerParams(vmem_limit_bytes=vmem * MIB),
        cost_estimate=pl.CostEstimate(
            flops=flops, bytes_accessed=bytes_accessed, transcendentals=0
        ),
    )(*args)


def dot(a, b, ca=1, cb=0):
    return lax.dot_general(a, b, (((ca,), (cb,)), ((), ())), preferred_element_type=F32)


def shift(array, axis, by, size=4):
    return lax.ppermute(array, axis, [((i + by) % size, i) for i in range(size)])


def x_shift(array, by):
    def rank(x):
        return (x % 2) * 2 + x // 2

    pairs = [(rank((x + by) % 4), rank(x)) for x in range(4)]
    return lax.ppermute(array, ("section", "xh"), pairs)


def swap(array, axis):
    return lax.ppermute(array, axis, [(0, 1), (1, 0)])


def gather_rows(rows):
    mine = jnp.concatenate([rows] + [shift(rows, "z", j) for j in (1, 2, 3)])
    return mine, swap(mine, "tensor")


def add_body(mine_ref, other_ref, *outs):
    for j, out in enumerate(outs):
        rows = pl.ds(64 * j, 64)
        total = mine_ref[rows, :].astype(F32) + other_ref[rows, :].astype(F32)
        out[...] = total.astype(out.dtype)


def scatter_rows(mine, other):
    arrived = swap(other, "tensor")
    blocks = call(
        add_body, [((64, D), F32)] + [((64, D), BF)] * 3, mine, arrived, bytes_accessed=MIB
    )
    return [blocks[0]] + [shift(blocks[j], "z", -j) for j in (1, 2, 3)]


def norm_stats(values):
    centred = values - jnp.mean(values, axis=-1, keepdims=True)
    rstd = lax.rsqrt(jnp.mean(centred * centred, axis=-1, keepdims=True) + EPS)
    return centred * rstd, rstd


def norm_back(grad, unit, rstd, gain):
    scaled = grad * gain
    return rstd * (
        scaled
        - jnp.mean(scaled, axis=-1, keepdims=True)
        - unit * jnp.mean(scaled * unit, axis=-1, keepdims=True)
    )


def total_of(refs):
    total = refs[0][...]
    for ref in refs[1:]:
        total = total + ref[...].astype(F32)
    return total


def first_norm_body(x_ref, par_ref, out_ref):
    unit, _ = norm_stats(x_ref[...].astype(F32))
    par = par_ref[...].astype(F32)
    out_ref[...] = (unit * par[0:1] + par[2:3]).astype(BF)


def mid_body(x_ref, b0, b1, b2, b3, par_ref, hidden_ref, out_ref):
    par = par_ref[...].astype(F32)
    hidden = x_ref[...].astype(F32) + total_of((b0, b1, b2, b3)) + par[4:5]
    hidden_ref[...] = hidden
    unit, _ = norm_stats(hidden)
    out_ref[...] = (unit * par[1:2] + par[3:4]).astype(BF)


def end_body(hidden_ref, b0, b1, b2, b3, par_ref, next_ref, act_ref, *out_ref):
    par = par_ref[...].astype(F32)
    act = (hidden_ref[...] + total_of((b0, b1, b2, b3)) + par[5:6]).astype(BF)
    act_ref[...] = act
    if out_ref:
        unit, _ = norm_stats(act.astype(F32))
        later = next_ref[...].astype(F32)
        out_ref[0][...] = (unit * later[0:1] + later[2:3]).astype(BF)


def head_lanes(h):
    lane = lax.broadcasted_iota(jnp.int32, (1, 2 * HD), 1)
    return (lane >= h * HD) & (lane < (h + 1) * HD)


def allowed_mask(column_ref, row_ref):
    return (row_ref[0:1, :] <= column_ref[:, 0:1]) & (row_ref[1:2, :] == column_ref[:, 1:2])


def attend_body(mine, other, w_ref, bias_ref, column_ref, row_ref, out_mine, out_other, qkv_ref, att_ref, low_ref):
    w = w_ref[:, : 3 * 128]
    rows = jnp.concatenate([mine[...], other[...]])
    projected = dot(rows, w)
    q = (projected[:, :128] + bias_ref[0:1, :]).astype(BF)
    k = projected[:, 128:256].astype(BF)
    v = (projected[:, 256:] + bias_ref[1:2, :]).astype(BF)
    qkv_ref[0] = q
    qkv_ref[1] = k
    qkv_ref[2] = v
    allowed = allowed_mask(column_ref, row_ref)
    zero = jnp.zeros((), BF)
    attended = jnp.zeros((RUN, 128), F32)
    for h in range(2):
        lanes = head_lanes(h)
        scores = dot(jnp.where(lanes, q, zero), k, 1, 1) * HD**-0.5
        scores = jnp.where(allowed, scores, MASKED)
        weights = jnp.where(
            allowed, jnp.exp(scores - jnp.max(scores, axis=-1, keepdims=True)), 0.0
        )
        total = jnp.sum(weights, axis=-1, keepdims=True)
        attended += dot(weights.astype(BF), jnp.where(lanes, v, zero)) / total
    att_ref[...] = attended
    low = attended.astype(BF)
    low_ref[...] = low
    part = dot(low, w_ref[:, 384:512], 1, 1)
    out_mine[...] = part[:256].astype(BF)
    out_other[...] = part[256:].astype(BF)


def attend_back_body(mine, other, w_ref, column_ref, row_ref, qkv_ref, att_ref, out_mine, out_other, grad_ref, sum_ref):
    w = w_ref[:, : 3 * 128]
    grad_low = dot(jnp.concatenate([mine[...], other[...]]), w_ref[:, 384:512]).astype(BF)
    grad_out = grad_low.astype(F32)
    q, k, v = qkv_ref[0], qkv_ref[1], qkv_ref[2]
    allowed = allowed_mask(column_ref, row_ref)
    zero = jnp.zeros((), BF)
    products = grad_out * att_ref[...]
    dq = jnp.zeros((RUN, 128), F32)
    dk = jnp.zeros((RUN, 128), F32)
    dv = jnp.zeros((RUN, 128), F32)
    for h in range(2):
        lanes = head_lanes(h)
        q_h = jnp.where(lanes, q, zero)
        scores = dot(q_h, k, 1, 1) * HD**-0.5
        scores = jnp.where(allowed, scores, MASKED)
        weights = jnp.where(
            allowed, jnp.exp(scores - jnp.max(scores, axis=-1, keepdims=True)), 0.0
        )
        inverse = 1.0 / jnp.sum(weights, axis=-1, keepdims=True)
        delta = jnp.sum(jnp.where(lanes, products, 0.0), axis=-1, keepdims=True)
        grad_h = jnp.where(lanes, grad_low, zero)
        grad_probs = dot(grad_h, v, 1, 1)
        grad_scores = (weights * inverse * (grad_probs - delta)).astype(BF)
        dq += dot(grad_scores, jnp.where(lanes, k, zero))
        dk += dot(grad_scores, q_h, 0, 0)
        scaled = (jnp.where(lanes, grad_out, 0.0) * inverse).astype(BF)
        dv += dot(weights.astype(BF), scaled, 0, 0)
    dq = (dq * HD**-0.5).astype(BF)
    dk = (dk * HD**-0.5).astype(BF)
    dv = dv.astype(BF)
    grads = jnp.concatenate([dq, dk, dv], axis=1)
    grad_ref[...] = grads
    sum_ref[0:1, :] = jnp.sum(dq.astype(F32), axis=0, keepdims=True)
    sum_ref[1:2, :] = jnp.sum(dv.astype(F32), axis=0, keepdims=True)
    part = dot(grads, w, 1, 1)
    out_mine[...] = part[:256].astype(BF)
    out_other[...] = part[256:].astype(BF)


def gelu_parts(u):
    cubic = 0.044715 * u * u
    t = jnp.tanh(0.7978845608028654 * u * (1.0 + cubic))
    return t, cubic


def feed_body(mine, other, w_ref, bias_ref, out_mine, out_other, u_ref, z_ref):
    rows = jnp.concatenate([mine[...], other[...]])
    u = dot(rows, w_ref[:, :512]) + bias_ref[...]
    u_ref[...] = u
    t, _ = gelu_parts(u)
    z = (0.5 * u * (1.0 + t)).astype(BF)
    z_ref[...] = z
    part = dot(z, w_ref[:, 512:], 1, 1)
    out_mine[...] = part[:256].astype(BF)
    out_other[...] = part[256:].astype(BF)


def feed_back_body(mine, other, w_ref, u_ref, out_mine, out_other, du_ref, sum_ref):
    grad_z = dot(jnp.concatenate([mine[...], other[...]]), w_ref[:, 512:])
    u = u_ref[...]
    t, cubic = gelu_parts(u)
    slope = 0.5 * (1.0 + t) + 0.5 * u * (1.0 - t * t) * 0.7978845608028654 * (1.0 + 3.0 * cubic)
    du = (grad_z * slope).astype(BF)
    du_ref[...] = du
    sum_ref[...] = jnp.sum(du.astype(F32), axis=0, keepdims=True)
    part = dot(du, w_ref[:, :512], 1, 1)
    out_mine[...] = part[:256].astype(BF)
    out_other[...] = part[256:].astype(BF)


def mid_back_body(g_ref, hidden_ref, b0, b1, b2, b3, par_ref, dh_ref, low_ref, sums_ref):
    g = g_ref[...].astype(F32)
    par = par_ref[...].astype(F32)
    grad = total_of((b0, b1, b2, b3))
    unit, rstd = norm_stats(hidden_ref[...])
    dh = g + norm_back(grad, unit, rstd, par[1:2])
    low = dh.astype(BF)
    dh_ref[...] = dh
    low_ref[...] = low
    sums_ref[0:1, :] = jnp.sum(grad * unit, axis=0, keepdims=True)
    sums_ref[1:2, :] = jnp.sum(grad, axis=0, keepdims=True)
    sums_ref[2:3, :] = jnp.sum(low.astype(F32), axis=0, keepdims=True)
    sums_ref[3:4, :] = jnp.sum(g, axis=0, keepdims=True)


def end_back_body(dh_ref, x_ref, b0, b1, b2, b3, par_ref, out_ref, sums_ref):
    par = par_ref[...].astype(F32)
    grad = total_of((b0, b1, b2, b3))
    unit, rstd = norm_stats(x_ref[...].astype(F32))
    out_ref[...] = (dh_ref[...] + norm_back(grad, unit, rstd, par[0:1])).astype(BF)
    sums_ref[0:1, :] = jnp.sum(grad * unit, axis=0, keepdims=True)
    sums_ref[1:2, :] = jnp.sum(grad, axis=0, keepdims=True)


def outer_body(a_mine, a_other, b_ref, out_ref):
    out_ref[...] = (dot(a_mine[...], b_ref[:256], 0, 0) + dot(a_other[...], b_ref[256:], 0, 0)).astype(BF)


def outer(halves, right):
    n = right.shape[1]
    return call(
        outer_body, [((D, n), BF)], *halves, right, flops=2 * RUN * D * n, bytes_accessed=2 * MIB
    )[0]


def place_body(index_ref, *refs):
    out = refs[-1]
    for j, ref in enumerate(refs[:-1]):
        out[:, lax.rem(index_ref[0] + j, 4)] = ref[...]


def place(index, pieces):
    lead, rows, columns = pieces[0].shape
    return call(
        place_body,
        [((lead, 4, rows, columns), pieces[0].dtype)],
        index.reshape(1),
        *pieces,
        scalars=1,
        bytes_accessed=16 * lead * rows * columns,
    )[0]


def quarter(array):
    return jnp.transpose(array.reshape(array.shape[0], 4, -1), (1, 0, 2))


def fetch_weights(qkv_weight, out_weight, up_weight, down_weight, qv_bias, up_bias, me):
    section, xh, y, z = me
    side = jnp.concatenate(
        [
            jnp.transpose(qv_bias[0].reshape(2, 4, 4), (1, 0, 2)).reshape(4, 1, 8),
            up_bias[0].reshape(4, 1, 16),
        ],
        axis=2,
    )
    packed = jnp.concatenate(
        [quarter(qkv_weight[0, j]) for j in range(3)]
        + [quarter(out_weight[0].T), jnp.pad(side, ((0, 0), (0, 31), (0, SIDE - 24)))]
        + [quarter(up_weight[0]), quarter(down_weight[0].T)],
        axis=2,
    )
    pieces = [lax.dynamic_index_in_dim(packed, z, 0)]
    for j in (1, 2, 3):
        to_send = lax.dynamic_index_in_dim(packed, lax.rem(z + 4 - j, 4), 0)
        pieces.append(shift(to_send, "z", j))
    own = place(z, pieces).reshape(128, ATT + SIDE + MLP)
    parts = []
    for part in (own[:, : ATT + SIDE], own[:, ATT + SIDE :]):
        right, left, across = x_shift(part, 1), x_shift(part, 3), x_shift(part, 2)
        layers = []
        for layer in (0, 1):
            near = jnp.where(section == layer, part, right if layer else left)
            far = jnp.where(section == layer, across, left if layer else right)
            layers.append(
                jnp.stack([jnp.where(xh == 0, near, far), jnp.where(xh == 0, far, near)])
            )
        parts.append(layers)
    weights = []
    for layer in (0, 1):
        held = []
        for part in parts:
            rows = part[layer]
            if layer == 0:
                full = place(y, [rows] + [shift(rows, "y", j) for j in (1, 2, 3)])
            else:
                full = lax.all_gather(rows, "y", axis=1)
            held.append(full.reshape(D, -1))
        att, feed = held
        side = att.reshape(32, 32, ATT + SIDE)[:, 0, ATT : ATT + 24].T.astype(F32)
        weights.append((att, feed, side[:8].reshape(2, 128), side[8:].reshape(1, 512)))
    return weights


def reduce_y(grad, y):
    blocks = grad.reshape(2, 4, 128, -1)
    total = lax.dynamic_index_in_dim(blocks, y, 1, keepdims=False).astype(F32)
    for j in (1, 2, 3):
        block = lax.dynamic_index_in_dim(blocks, lax.rem(y + j, 4), 1, keepdims=False)
        total = total + shift(block, "y", -j).astype(F32)
    return total


def reduce_x(totals, me):
    section, xh, _, _ = me

    def block(layer, half):
        return lax.dynamic_index_in_dim(
            jnp.where(layer == 0, totals[0], totals[1]), half, 0, keepdims=False
        )

    x = xh * 2 + section
    total = block(section, xh)
    for j in (1, 2, 3):
        to = lax.rem(x + j, 4)
        total = total + x_shift(block(lax.rem(to, 2), to // 2).astype(BF), -j).astype(F32)
    return total


def spread_z(total, z):
    blocks = total.astype(BF).reshape(4, 32, -1)
    pieces = [lax.dynamic_index_in_dim(blocks, z, 0)]
    for j in (1, 2, 3):
        to_send = lax.dynamic_index_in_dim(blocks, lax.rem(z + 4 - j, 4), 0)
        pieces.append(shift(to_send, "z", j))
    return place(z, pieces)[0].astype(F32)


def widen(array):
    return jnp.transpose(array, (1, 0, 2)).reshape(array.shape[1], -1)


def shards(inputs, cotangent, segments, qkv_weight, out_weight, up_weight, down_weight, norm_gains, biases, qv_bias, up_bias):
    section, xh, y, z = (lax.axis_index(name) for name in ("section", "xh", "y", "z"))
    core = lax.axis_index("tensor")
    me = (section, xh, y, z)
    x0 = lax.dynamic_index_in_dim(inputs, section, 0, keepdims=False)
    g1 = lax.dynamic_index_in_dim(cotangent, section, 0, keepdims=False)
    own_par = jnp.concatenate([norm_gains[0], biases[0]])
    other_par = swap(own_par, "section")
    pars = [
        jnp.where(section == 0, own_par, other_par),
        jnp.where(section == 0, other_par, own_par),
    ]
    weights = fetch_weights(qkv_weight, out_weight, up_weight, down_weight, qv_bias, up_bias, me)

    order = jnp.arange(RUN, dtype=jnp.int32)
    place_in_run = (
        lax.rem(z + lax.rem(order // 64, 4), 4) * 128
        + jnp.where(order < 256, core, 1 - core) * 64
        + lax.rem(order, 64)
    )
    row = lax.dynamic_index_in_dim(segments, section, 0, keepdims=False)
    run_segments = lax.dynamic_slice_in_dim(row, (xh * 4 + y) * RUN, RUN)
    marks = jnp.stack([place_in_run, run_segments[place_in_run]])
    mark_row = jnp.pad(marks, ((0, 6), (0, 0)))
    mark_column = jnp.pad(marks.T, ((0, 0), (0, 126)))

    big = 4 * MIB
    half = [((256, D), BF)] * 2
    saved = []
    acts = []
    rows = x0
    normed = call(first_norm_body, [((64, D), BF)], x0, pars[0])[0]
    for layer in (0, 1):
        att, feed, qv, upb = weights[layer]
        par = pars[layer]
        a_rows = gather_rows(normed)
        *parts, qkv, attended, att_low = call(
            attend_body,
            half + [((3, RUN, 128), BF), ((RUN, 128), F32), ((RUN, 128), BF)],
            *a_rows, att, qv, mark_column, mark_row,
            flops=2 * RUN * (D * 512 + 4 * RUN * 128), bytes_accessed=big,
        )
        hidden, second = call(
            mid_body, [((64, D), F32), ((64, D), BF)], rows, *scatter_rows(*parts), par
        )
        b_rows = gather_rows(second)
        *parts, u, gelu_low = call(
            feed_body,
            half + [((RUN, 512), F32), ((RUN, 512), BF)],
            *b_rows, feed, upb,
            flops=4 * RUN * D * 512, bytes_accessed=big,
        )
        saved.append((rows, a_rows, qkv, attended, att_low, hidden, b_rows, u, gelu_low))
        ended = call(
            end_body,
            [((64, D), BF)] * (2 - layer),
            hidden, *scatter_rows(*parts), par, pars[1],
        )
        acts.append(ended[0])
        rows = ended[0]
        normed = ended[-1]

    grads = [None, None]
    grad_rows = g1
    vectors = [None, None]
    sides = [None, None]
    inputs_back = [None, None]
    for layer in (1, 0):
        att, feed, qv, upb = weights[layer]
        par = pars[layer]
        rows, a_rows, qkv, attended, att_low, hidden, b_rows, u, gelu_low = saved[layer]
        g_rows = gather_rows(grad_rows)
        *parts, du, u_sum = call(
            feed_back_body,
            half + [((RUN, 512), BF), ((1, 512), F32)],
            *g_rows, feed, u,
            flops=4 * RUN * D * 512, bytes_accessed=big,
        )
        grad_down = outer(g_rows, gelu_low)
        grad_up = outer(b_rows, du)
        dh, dh_low, sums_two = call(
            mid_back_body,
            [((64, D), F32), ((64, D), BF), ((4, D), F32)],
            grad_rows, hidden, *scatter_rows(*parts), par,
        )
        h_rows = gather_rows(dh_low)
        *parts, dqkv, qv_sum = call(
            attend_back_body,
            half + [((RUN, 384), BF), ((2, 128), F32)],
            *h_rows, att, mark_column, mark_row, qkv, attended,
            flops=2 * RUN * (D * 512 + 10 * RUN * 128), bytes_accessed=big,
        )
        grad_out = outer(h_rows, att_low)
        grad_qkv = outer(a_rows, dqkv)
        grad_rows, sums_one = call(
            end_back_body,
            [((64, D), BF), ((2, D), F32)],
            dh, rows, *scatter_rows(*parts), par,
        )
        inputs_back[layer] = grad_rows
        grads[layer] = (grad_qkv, grad_out, grad_up, grad_down)
        vectors[layer] = jnp.concatenate(
            [sums_one[0:1], sums_two[0:1], sums_one[1:2], sums_two[1:]]
        )
        sides[layer] = jnp.pad(
            jnp.concatenate([qv_sum.reshape(1, 256), u_sum], axis=1), ((0, 0), (0, D - 768))
        )

    totals = []
    for layer in (0, 1):
        totals.append(
            jnp.concatenate([reduce_y(grad, y) for grad in grads[layer]], axis=-1)
        )
    mine = spread_z(reduce_x(totals, me), z)
    grad_qkv = jnp.stack([widen(mine[:, :, 128 * j : 128 * j + 128]) for j in range(3)])
    grad_out = widen(mine[:, :, 384:512]).T
    grad_up = widen(mine[:, :, 512:1024])
    grad_down = widen(mine[:, :, 1024:]).T

    small = jnp.concatenate(vectors + sides + [jnp.zeros((2, D), F32)])
    small = small + (x_shift(small, 1) + x_shift(small, 2) + x_shift(small, 3))
    small = small + (shift(small, "y", 1) + shift(small, "y", 2) + shift(small, "y", 3))
    along = [small] + [shift(small, "z", j) for j in (1, 2, 3)]
    vector = (along[0] + along[1]) + (along[2] + along[3])
    vector = jnp.where(section == 0, vector[0:6], vector[6:12])
    vector = vector + swap(vector, "tensor")
    side = place(z, [jnp.where(section == 0, a[12:13], a[13:14]).reshape(1, 1, D) for a in along])
    side = side.reshape(4, D)
    index = (xh * 4 + y) * 4 + z

    def column(array):
        return lax.dynamic_index_in_dim(array.reshape(-1, VEC), index, 1, keepdims=True)

    grad_qv = jnp.stack([column(side[:, :128]), column(side[:, 128:256])])
    grad_upb = column(side[:, 256:768])

    def own_layer(per_layer):
        kept = jnp.where(section == 0, per_layer[0], per_layer[1])
        sent = swap(jnp.where(section == 0, per_layer[1], per_layer[0]), "section")
        return jnp.stack(
            [jnp.where(section == 0, kept, sent), jnp.where(section == 0, sent, kept)]
        )[None]

    return (
        own_layer(acts),
        own_layer(inputs_back),
        grad_qkv[None],
        grad_out[None],
        grad_up[None],
        grad_down[None],
        vector[None, 0:2],
        vector[None, 2:6],
        grad_qv[None],
        grad_upb[None],
    )


def solution(mesh):
    fine = Mesh(mesh.devices.reshape(2, 2, 4, 4, 2), ("section", "xh", "y", "z", "tensor"))
    dp = ("xh", "y", "z")
    return jax.shard_map(
        shards,
        mesh=fine,
        in_specs=(
            P(None, (*dp, "tensor"), None),
            P(None, (*dp, "tensor"), None),
            P(),
            P("section", None, dp, "tensor"),
            P("section", "tensor", dp),
            P("section", dp, "tensor"),
            P("section", "tensor", dp),
            P("section", None, None),
            P("section", None, None),
            P("section", None, "tensor", dp),
            P("section", "tensor", dp),
        ),
        out_specs=(
            P("section", None, (*dp, "tensor"), None),
            P("section", None, (*dp, "tensor"), None),
            P("section", None, dp, "tensor"),
            P("section", "tensor", dp),
            P("section", dp, "tensor"),
            P("section", "tensor", dp),
            P("section", None, None),
            P("section", None, None),
            P("section", None, "tensor", dp),
            P("section", "tensor", dp),
        ),
        check_vma=False,
    )
```

```python
import jax
import jax.numpy as jnp
from jax import lax
from jax.experimental import pallas as pl
from jax.experimental.pallas import tpu as pltpu
from jax.sharding import Mesh, PartitionSpec as P

D = 1024
HD = 64
VEC = 32
RUN = 512
EPS = 1e-05
MASKED = -1e30
BF = jnp.bfloat16
F32 = jnp.float32
ATT = 512
MLP = 1024
MIB = 1024 * 1024


def call(body, outs, *args, flops=0, scalars=0, after=(), vmem=16):
    specs = [pl.BlockSpec(memory_space=pltpu.SMEM)] * scalars
    specs += [pl.BlockSpec(memory_space=pltpu.VMEM)] * (len(args) - scalars)
    specs += [pl.BlockSpec(memory_space=pl.ANY)] * len(after)
    count = len(args)

    def kernel(*refs):
        body(*refs[:count], *refs[count + len(after) :])

    return pl.pallas_call(
        kernel,
        out_shape=[jax.ShapeDtypeStruct(shape, dtype) for shape, dtype in outs],
        in_specs=specs,
        out_specs=[pl.BlockSpec(memory_space=pltpu.VMEM)] * len(outs),
        compiler_params=pltpu.CompilerParams(vmem_limit_bytes=vmem * MIB),
        cost_estimate=pl.CostEstimate(
            flops=flops, bytes_accessed=MIB // 8, transcendentals=0
        ),
    )(*args, *after)


def dot(a, b, ca=1, cb=0):
    return lax.dot_general(a, b, (((ca,), (cb,)), ((), ())), preferred_element_type=F32)


def shift(array, axis, by, size=4):
    return lax.ppermute(array, axis, [((i + by) % size, i) for i in range(size)])


def x_shift(array, by):
    def rank(x):
        return (x % 2) * 2 + x // 2

    pairs = [(rank((x + by) % 4), rank(x)) for x in range(4)]
    return lax.ppermute(array, ("section", "xh"), pairs)


def swap(array, axis):
    return lax.ppermute(array, axis, [(0, 1), (1, 0)])


def gather_rows(rows):
    across, *sides = [shift(rows, "z", j) for j in (2, 1, 3)]
    mine = [rows, sides[0], across, sides[1]]
    return mine + [swap(piece, "tensor") for piece in mine]


def whole(refs):
    return jnp.concatenate([ref[...] for ref in refs])


def add_body(mine_ref, other_ref, *outs):
    for j, out in enumerate(outs):
        rows = pl.ds(64 * j, 64)
        total = mine_ref[rows, :].astype(F32) + other_ref[rows, :].astype(F32)
        out[...] = total.astype(out.dtype)


def scatter_rows(mine, other):
    arrived = swap(other, "tensor")
    blocks = call(
        add_body, [((64, D), F32)] + [((64, D), BF)] * 3, mine, arrived
    )
    return [blocks[0]] + [shift(blocks[j], "z", -j) for j in (2, 1, 3)], blocks[1]


def norm_stats(values):
    centred = values - jnp.mean(values, axis=-1, keepdims=True)
    rstd = lax.rsqrt(jnp.mean(centred * centred, axis=-1, keepdims=True) + EPS)
    return centred * rstd, rstd


def norm_back(grad, unit, rstd, gain):
    scaled = grad * gain
    return rstd * (
        scaled
        - jnp.mean(scaled, axis=-1, keepdims=True)
        - unit * jnp.mean(scaled * unit, axis=-1, keepdims=True)
    )


def total_of(refs):
    total = refs[0][...]
    for ref in refs[1:]:
        total = total + ref[...].astype(F32)
    return total


def first_norm_body(x_ref, par_ref, out_ref):
    unit, _ = norm_stats(x_ref[...].astype(F32))
    par = par_ref[...].astype(F32)
    out_ref[...] = (unit * par[0:1] + par[2:3]).astype(BF)


def mid_body(x_ref, b0, b1, b2, b3, par_ref, hidden_ref, out_ref):
    par = par_ref[...].astype(F32)
    hidden = x_ref[...].astype(F32) + total_of((b0, b1, b2, b3)) + par[4:5]
    hidden_ref[...] = hidden
    unit, _ = norm_stats(hidden)
    out_ref[...] = (unit * par[1:2] + par[3:4]).astype(BF)


def end_body(hidden_ref, b0, b1, b2, b3, par_ref, next_ref, act_ref, *out_ref):
    par = par_ref[...].astype(F32)
    act = (hidden_ref[...] + total_of((b0, b1, b2, b3)) + par[5:6]).astype(BF)
    act_ref[...] = act
    if out_ref:
        unit, _ = norm_stats(act.astype(F32))
        later = next_ref[...].astype(F32)
        out_ref[0][...] = (unit * later[0:1] + later[2:3]).astype(BF)


def head_lanes(h):
    lane = lax.broadcasted_iota(jnp.int32, (1, 2 * HD), 1)
    return (lane >= h * HD) & (lane < (h + 1) * HD)


def column_bias(side_ref, first, count):
    side = side_ref[...].reshape(8, 16, 128)[:, :4].reshape(32, 128)
    n = 32 * count
    lane = lax.broadcasted_iota(jnp.int32, (128, n), 0)
    entry = lax.broadcasted_iota(jnp.int32, (128, n), 1)
    spread = dot(side, (lane == first + entry // 32).astype(F32))
    device = lax.broadcasted_iota(jnp.int32, (32, n), 0)
    entry = lax.broadcasted_iota(jnp.int32, (32, n), 1)
    return jnp.sum(jnp.where(entry % 32 == device, spread, 0.0), axis=0, keepdims=True)


def attend_body(*refs):
    rows = whole(refs[:8])
    w_ref, side_ref, mask_ref, out_mine, out_other, qkv_ref, att_ref, low_ref = refs[8:]
    projected = dot(rows, w_ref[:, : 3 * 128])
    q = (projected[:, :128] + column_bias(side_ref, 0, 4)).astype(BF)
    k = projected[:, 128:256].astype(BF)
    v = (projected[:, 256:] + column_bias(side_ref, 4, 4)).astype(BF)
    qkv_ref[0] = q
    qkv_ref[1] = k
    qkv_ref[2] = v
    zero = jnp.zeros((), BF)
    attended = jnp.zeros((RUN, 128), F32)
    for h in range(2):
        lanes = head_lanes(h)
        scores = dot(jnp.where(lanes, q, zero), k, 1, 1) * HD**-0.5 + mask_ref[...]
        weights = jnp.exp(scores - jnp.max(scores, axis=-1, keepdims=True))
        total = jnp.sum(weights, axis=-1, keepdims=True)
        attended += dot(weights.astype(BF), jnp.where(lanes, v, zero)) / total
    att_ref[...] = attended
    low = attended.astype(BF)
    low_ref[...] = low
    part = dot(low, w_ref[:, 384:512], 1, 1)
    out_mine[...] = part[:256].astype(BF)
    out_other[...] = part[256:].astype(BF)


def attend_back_body(*refs):
    rows = whole(refs[:8])
    w_ref, mask_ref, qkv_ref, att_ref, out_mine, out_other, grad_ref, sum_ref = refs[8:]
    grad_low = dot(rows, w_ref[:, 384:512]).astype(BF)
    grad_out = grad_low.astype(F32)
    q, k, v = qkv_ref[0], qkv_ref[1], qkv_ref[2]
    zero = jnp.zeros((), BF)
    products = grad_out * att_ref[...]
    dq = jnp.zeros((RUN, 128), F32)
    dk = jnp.zeros((RUN, 128), F32)
    dv = jnp.zeros((RUN, 128), F32)
    for h in range(2):
        lanes = head_lanes(h)
        q_h = jnp.where(lanes, q, zero)
        scores = dot(q_h, k, 1, 1) * HD**-0.5 + mask_ref[...]
        weights = jnp.exp(scores - jnp.max(scores, axis=-1, keepdims=True))
        inverse = 1.0 / jnp.sum(weights, axis=-1, keepdims=True)
        delta = jnp.sum(jnp.where(lanes, products, 0.0), axis=-1, keepdims=True)
        grad_h = jnp.where(lanes, grad_low, zero)
        grad_probs = dot(grad_h, v, 1, 1)
        grad_scores = (weights * inverse * (grad_probs - delta)).astype(BF)
        dq += dot(grad_scores, jnp.where(lanes, k, zero))
        dk += dot(grad_scores, q_h, 0, 0)
        scaled = (jnp.where(lanes, grad_out, 0.0) * inverse).astype(BF)
        dv += dot(weights.astype(BF), scaled, 0, 0)
    dq = (dq * HD**-0.5).astype(BF)
    dk = (dk * HD**-0.5).astype(BF)
    dv = dv.astype(BF)
    grads = jnp.concatenate([dq, dk, dv], axis=1)
    grad_ref[...] = grads
    sum_ref[0:1, :] = jnp.sum(dq.astype(F32), axis=0, keepdims=True)
    sum_ref[1:2, :] = jnp.sum(dv.astype(F32), axis=0, keepdims=True)
    part = dot(grads, w_ref[:, : 3 * 128], 1, 1)
    out_mine[...] = part[:256].astype(BF)
    out_other[...] = part[256:].astype(BF)


def gelu_parts(u):
    cubic = 0.044715 * u * u
    t = jnp.tanh(0.7978845608028654 * u * (1.0 + cubic))
    return t, cubic


def feed_body(*refs):
    rows = whole(refs[:8])
    w_ref, side_ref, out_mine, out_other, u_ref, z_ref = refs[8:]
    u = dot(rows, w_ref[:, :512]) + column_bias(side_ref, 8, 16)
    u_ref[...] = u
    t, _ = gelu_parts(u)
    z = (0.5 * u * (1.0 + t)).astype(BF)
    z_ref[...] = z
    part = dot(z, w_ref[:, 512:], 1, 1)
    out_mine[...] = part[:256].astype(BF)
    out_other[...] = part[256:].astype(BF)


def feed_back_body(*refs):
    rows = whole(refs[:8])
    w_ref, u_ref, out_mine, out_other, du_ref, sum_ref = refs[8:]
    grad_z = dot(rows, w_ref[:, 512:])
    u = u_ref[...]
    t, cubic = gelu_parts(u)
    slope = 0.5 * (1.0 + t) + 0.5 * u * (1.0 - t * t) * 0.7978845608028654 * (1.0 + 3.0 * cubic)
    du = (grad_z * slope).astype(BF)
    du_ref[...] = du
    sum_ref[...] = jnp.sum(du.astype(F32), axis=0, keepdims=True)
    part = dot(du, w_ref[:, :512], 1, 1)
    out_mine[...] = part[:256].astype(BF)
    out_other[...] = part[256:].astype(BF)


def mid_back_body(g_ref, hidden_ref, b0, b1, b2, b3, par_ref, dh_ref, low_ref, sums_ref):
    g = g_ref[...].astype(F32)
    par = par_ref[...].astype(F32)
    grad = total_of((b0, b1, b2, b3))
    unit, rstd = norm_stats(hidden_ref[...])
    dh = g + norm_back(grad, unit, rstd, par[1:2])
    low = dh.astype(BF)
    dh_ref[...] = dh
    low_ref[...] = low
    sums_ref[0:1, :] = jnp.sum(grad * unit, axis=0, keepdims=True)
    sums_ref[1:2, :] = jnp.sum(grad, axis=0, keepdims=True)
    sums_ref[2:3, :] = jnp.sum(low.astype(F32), axis=0, keepdims=True)
    sums_ref[3:4, :] = jnp.sum(g, axis=0, keepdims=True)


def end_back_body(dh_ref, x_ref, b0, b1, b2, b3, par_ref, out_ref, sums_ref):
    par = par_ref[...].astype(F32)
    grad = total_of((b0, b1, b2, b3))
    unit, rstd = norm_stats(x_ref[...].astype(F32))
    out_ref[...] = (dh_ref[...] + norm_back(grad, unit, rstd, par[0:1])).astype(BF)
    sums_ref[0:1, :] = jnp.sum(grad * unit, axis=0, keepdims=True)
    sums_ref[1:2, :] = jnp.sum(grad, axis=0, keepdims=True)


def feed_grads_body(*refs):
    g, b = whole(refs[:8]), whole(refs[8:16])
    du_ref, z_ref, out_ref = refs[16:]
    out_ref[:, :512] = dot(b, du_ref[...], 0, 0).astype(BF)
    out_ref[:, 512:] = dot(g, z_ref[...], 0, 0).astype(BF)


def y_messages(at_ref, outs, *columns):
    y = at_ref[3]
    for place in range(4):
        slot = lax.rem(place + 4 - y, 4)
        for j in range(4):

            @pl.when(slot == j)
            def _(out=outs[j], place=place):
                for half in range(2):
                    rows = slice((half * 4 + place) * 128, (half * 4 + place) * 128 + 128)
                    first = 0
                    for column in columns:
                        n = column.shape[1]
                        out[half * 128 : half * 128 + 128, first : first + n] = column[rows]
                        first += n


def feed_grads_body(at_ref, *refs):
    g, b = whole(refs[:8]), whole(refs[8:16])
    du_ref, z_ref = refs[16:18]
    up = dot(b, du_ref[...], 0, 0).astype(BF)
    down = dot(g, z_ref[...], 0, 0).astype(BF)
    y_messages(at_ref, refs[18:], up, down)


def attend_grads(a, h, dqkv, low):
    return dot(a, dqkv, 0, 0).astype(BF), dot(h, low, 0, 0).astype(BF)


def attend_grads_body(at_ref, *refs):
    dqkv_ref, low_ref = refs[16:18]
    columns = attend_grads(whole(refs[:8]), whole(refs[8:16]), dqkv_ref[...], low_ref[...])
    y_messages(at_ref, refs[18:], *columns)


def sum_body(*refs):
    refs[-1][...] = sum_of(refs[:-1]).astype(BF)


def pack_body(at_ref, qkv_ref, out_ref, up_ref, down_ref, qv_ref, upb_ref, *refs):
    qv = qv_ref[...].astype(F32)
    upb = upb_ref[...].astype(F32)

    def pick(row, first, count, start):
        n = row.shape[1]
        entry = lax.broadcasted_iota(jnp.int32, (n, 128), 0)
        lane = lax.broadcasted_iota(jnp.int32, (n, 128), 1)
        chosen = (entry == start + lane - first) & (lane >= first) & (lane < first + count)
        return dot(jnp.broadcast_to(row, (16, n)), chosen.astype(F32))

    for j in range(4):
        to = lax.rem(at_ref[0] + j, 4)
        narrow = pl.ds(pl.multiple_of(to * 128, 128), 128)
        broad = pl.ds(pl.multiple_of(to * 512, 512), 512)
        att = refs[j]
        for i in range(3):
            att[:32, 128 * i : 128 * i + 128] = qkv_ref[i, :, narrow]
        att[:32, 384:] = out_ref[:, narrow]
        side = pick(qv[0:1], 0, 4, 4 * to) + pick(qv[1:2], 4, 4, 4 * to) + pick(upb, 8, 16, 16 * to)
        att[32:48, :128] = side.astype(BF)
        att[32:48, 128:] = jnp.zeros((16, 384), BF)
        att[48:80, :] = up_ref[:, broad]
        att[80:, :] = down_ref[:, broad]


def collect_body(at_ref, *refs):
    att_ref, feed_ref = refs[4:]
    row = lax.broadcasted_iota(jnp.int32, (16, 512), 0)
    side = jnp.zeros((16, 512), F32)
    for j in range(4):
        place = lax.rem(at_ref[0] + 4 - j, 4)
        rows = pl.ds(pl.multiple_of(place * 32, 32), 32)
        att_ref[rows, :] = refs[j][:32, :]
        feed_ref[rows, :512] = refs[j][48:80, :]
        feed_ref[rows, 512:] = refs[j][80:, :]
        side = jnp.where(row == place, refs[j][32:48, :].astype(F32), side)
    att_ref[128:, :] = side.astype(BF)


def select_body(layers, at_ref, own, right, left, across, *outs):
    section, xh = at_ref[1], at_ref[2]
    for layer, out in zip(layers, outs):
        near = jnp.where(section == layer, own[...], (right if layer else left)[...])
        far = jnp.where(section == layer, across[...], (left if layer else right)[...])
        out[xh] = near
        out[1 - xh] = far


def place_y_body(at_ref, *refs):
    out = refs[4]
    for j in range(4):
        place = lax.rem(at_ref[3] + j, 4)
        for half in range(2):
            rows = pl.ds(pl.multiple_of((half * 4 + place) * 128, 128), 128)
            out[rows, :] = refs[j][half, :128, :]
            if len(refs) > 5:
                rows = pl.ds(pl.multiple_of((half * 4 + place) * 16, 16), 16)
                refs[5][rows, :] = refs[j][half, 128:, :128]


def last_grads_body(at_ref, *refs):
    a, h = whole(refs[:8]), whole(refs[8:16])
    dqkv_ref, low_ref, mine, other, par_ref, two0, one1, two1, qv0, u0, qv1, u1 = refs[16:28]
    outs = refs[28:32]
    sums = refs[32]
    par = par_ref[...].astype(F32)
    part = jnp.concatenate([mine[...], other[...]]).astype(F32)
    unit = (a.astype(F32) - par[2:3]) / par[0:1]
    sums[...] = jnp.zeros((16, D), F32)
    sums[0:1, :] = jnp.sum(part * unit, axis=0, keepdims=True)
    sums[1:2, :] = two0[0:1, :]
    sums[2:3, :] = jnp.sum(part, axis=0, keepdims=True)
    sums[3:6, :] = two0[1:4, :]
    sums[6:7, :] = one1[0:1, :]
    sums[7:8, :] = two1[0:1, :]
    sums[8:9, :] = one1[1:2, :]
    sums[9:12, :] = two1[1:4, :]
    for row, qv, u in ((12, qv0, u0), (13, qv1, u1)):
        sums[row : row + 1, :128] = qv[0:1, :]
        sums[row : row + 1, 128:256] = qv[1:2, :]
        sums[row : row + 1, 256:768] = u[...]
    first, second = attend_grads(a, h, dqkv_ref[...], low_ref[...])
    low = sums[...].astype(BF)
    y_messages(at_ref, outs, first, second)
    for out in outs:
        out[256:272, :] = low[:, :512]
        out[272:288, :] = low[:, 512:]


def sum_of(refs):
    total = refs[0][...].astype(F32)
    for ref in refs[1:]:
        total = total + ref[...].astype(F32)
    return total


def target_x(at_ref, j):
    x = lax.rem(at_ref[2] * 2 + at_ref[1] + j, 4)
    return lax.rem(x, 2), x // 2


def feed_blocks_body(at_ref, first, second, *outs):
    for j, out in enumerate(outs):
        layer, half = target_x(at_ref, j)
        rows = pl.ds(pl.multiple_of(half * 128, 128), 128)
        out[...] = jnp.where(layer == 0, first[rows, :], second[rows, :])


def attend_blocks_body(at_ref, m0, m1, m2, m3, second, *outs):
    total = sum_of((m0, m1, m2, m3))
    low = total.astype(BF)
    for j, out in enumerate(outs):
        layer, half = target_x(at_ref, j)
        own = jnp.where(half == 0, low[:128], low[128:256])
        rows = pl.ds(pl.multiple_of(half * 128, 128), 128)
        out[:128, :] = jnp.where(layer == 0, own, second[rows, :])
        out[128:, :] = low[256:]


def z_blocks_body(at_ref, a0, a1, a2, a3, f0, f1, f2, f3, o0, o1, o2, o3, rows_ref):
    att = sum_of((a0, a1, a2, a3)).astype(BF)
    rows_ref[:, :512] = att[:128]
    rows_ref[:, 512:] = sum_of((f0, f1, f2, f3)).astype(BF)
    for j, out in enumerate((o0, o1, o2, o3)):
        to = lax.rem(at_ref[0] + j, 4)
        out[:32, :] = rows_ref[pl.ds(pl.multiple_of(to * 32, 32), 32), :]
        out[32:, :512] = att[128:144]
        out[32:, 512:1024] = att[144:160]
        out[32:, 1024:] = jnp.zeros((16, 512), BF)


def finish_body(at_ref, m0, m1, m2, m3, qkv_ref, out_ref, up_ref, down_ref, vector_ref, side_ref):
    row = lax.broadcasted_iota(jnp.int32, (8, 768), 0)
    total = jnp.zeros((16, D), F32)
    side = jnp.zeros((8, 768), F32)
    section = at_ref[1]
    for j, ref in enumerate((m0, m1, m2, m3)):
        place = lax.rem(at_ref[0] + 4 - j, 4)
        narrow = pl.ds(pl.multiple_of(place * 128, 128), 128)
        broad = pl.ds(pl.multiple_of(place * 512, 512), 512)
        for i in range(3):
            qkv_ref[i, :, narrow] = ref[:32, 128 * i : 128 * i + 128].astype(F32)
        out_ref[:, narrow] = ref[:32, 384:512].astype(F32)
        up_ref[:, broad] = ref[:32, 512:1024].astype(F32)
        down_ref[:, broad] = ref[:32, 1024:].astype(F32)
        sums = ref[32:, :1024].astype(F32)
        total = total + sums
        own = jnp.where(section == 0, sums[12:13, :768], sums[13:14, :768])
        side = jnp.where(row == place, own, side)
    vector_ref[...] = jnp.where(section == 0, total[:6], total[6:12])
    index = (at_ref[2] * 4 + at_ref[3]) * 4 + at_ref[0]
    entry = lax.broadcasted_iota(jnp.int32, (8, 768), 1)
    kept = jnp.where(entry % 32 == index, side, 0.0)
    entry = lax.broadcasted_iota(jnp.int32, (768, 128), 0)
    lane = lax.broadcasted_iota(jnp.int32, (768, 128), 1)
    side_ref[...] = dot(kept, (entry // 32 == lane).astype(F32))


def shards(inputs, cotangent, segments, qkv_weight, out_weight, up_weight, down_weight, norm_gains, biases, qv_bias, up_bias):
    section, xh, y, z = (lax.axis_index(name) for name in ("section", "xh", "y", "z"))
    core = lax.axis_index("tensor")
    at = jnp.stack([z, section, xh, y]).astype(jnp.int32)
    x0 = lax.dynamic_index_in_dim(inputs, section, 0, keepdims=False)
    g1 = lax.dynamic_index_in_dim(cotangent, section, 0, keepdims=False)
    own_par = jnp.concatenate([norm_gains[0], biases[0]])
    other_par = swap(own_par, "section")

    packed = call(
        pack_body,
        [((112, ATT), BF)] * 4,
        at, qkv_weight[0], out_weight[0].T, up_weight[0], down_weight[0].T,
        qv_bias[0, :, :, 0], up_bias[0].T,
        scalars=1,
    )
    came = [packed[0]] + [shift(packed[j], "z", -j) for j in (1, 2, 3)]
    att_rows, feed_rows = call(
        collect_body, [((144, ATT), BF), ((128, MLP), BF)], at, *came, scalars=1
    )

    def along_x(part):
        return [part] + [x_shift(part, j) for j in (1, 3, 2)]

    def select(layers, pieces, after=()):
        outs = [((2, *pieces[0].shape), BF)] * len(layers)
        body = lambda *refs: select_body(layers, *refs)
        return call(body, outs, at, *pieces, scalars=1, after=after)

    def along_y(part):
        return [part] + [shift(part, "y", j) for j in (1, 2, 3)]

    def place_att(pieces, after):
        return call(
            place_y_body, [((D, ATT), BF), ((128, 128), BF)], at, *pieces, scalars=1, after=after
        )

    def place_feed(pieces, after):
        return call(place_y_body, [((D, MLP), BF)], at, *pieces, scalars=1, after=after)[0]

    att_x = along_x(att_rows)
    feed_x = along_x(feed_rows)

    row = lax.dynamic_index_in_dim(segments, section, 0, keepdims=False)
    run = lax.dynamic_slice_in_dim(row, (xh * 4 + y) * RUN, RUN)
    marks = jnp.stack([jnp.arange(RUN, dtype=jnp.int32), run]).reshape(2, 4, 2, 64)
    marks = lax.dynamic_slice_in_dim(jnp.concatenate([marks, marks], axis=1), z, 4, 1)
    marks = jnp.where(core == 0, marks, marks[:, :, ::-1])
    marks = jnp.transpose(marks, (0, 2, 1, 3)).reshape(2, RUN)
    allowed = (marks[0][None, :] <= marks[0][:, None]) & (marks[1][None, :] == marks[1][:, None])
    mask = jnp.where(allowed, 0.0, MASKED).astype(F32)

    pars = [
        jnp.where(section == 0, own_par, other_par),
        jnp.where(section == 0, other_par, own_par),
    ]
    g_first = gather_rows(g1)

    half = [((256, D), BF)] * 2
    saved = []
    acts = []
    weights = []
    rows = x0
    normed = call(first_norm_body, [((64, D), BF)], x0, pars[0])[0]
    (att,) = select((0,), att_x)
    att_y = along_y(att)
    for layer in (0, 1):
        par = pars[layer]
        a_rows = gather_rows(normed)
        att, side = place_att(att_y, after=a_rows[:4] + (a_rows[4:] if layer else [*g_first, mask]))
        (feed,) = select((layer,), feed_x, after=(att,))
        feed_y = along_y(feed)
        *parts, qkv, attended, att_low = call(
            attend_body,
            half + [((3, RUN, 128), BF), ((RUN, 128), F32), ((RUN, 128), BF)],
            *a_rows, att, side, mask, after=(feed,),
        )
        blocks, _ = scatter_rows(*parts)
        hidden, second = call(
            mid_body, [((64, D), F32), ((64, D), BF)], rows, *blocks, par
        )
        b_rows = gather_rows(second)
        feed = place_feed(feed_y, after=b_rows[:4])
        weights.append((att, feed))
        after = ()
        if layer == 0:
            (att,) = select((1,), att_x, after=(feed,))
            att_y = along_y(att)
            after = (att,)
        *parts, u, gelu_low = call(
            feed_body, half + [((RUN, 512), F32), ((RUN, 512), BF)], *b_rows, feed, side, after=after
        )
        saved.append((rows, a_rows, qkv, attended, att_low, hidden, b_rows, u, gelu_low))
        blocks, _ = scatter_rows(*parts)
        ended = call(
            end_body, [((64, D), BF)] * (2 - layer), hidden, *blocks, par, pars[1]
        )
        acts.append(ended[0])
        rows = ended[0]
        normed = ended[-1]

    grad_rows = g1
    g_rows = g_first
    inputs_back = [None, None]
    sums_two = [None, None]
    sums_one = [None, None]
    u_sum = [None, None]
    qv_sum = [None, None]
    feed_sums = [None, None]
    waiting = None

    def finish_y(messages, shape, after):
        arrived = [messages[0]] + [shift(messages[j], "y", -j) for j in (1, 2, 3)]
        return call(sum_body, [(shape, BF)], *arrived, after=after)[0]

    for layer in (1, 0):
        att, feed = weights[layer]
        par = pars[layer]
        rows, a_rows, qkv, attended, att_low, hidden, b_rows, u, gelu_low = saved[layer]
        if layer == 0:
            g_rows = gather_rows(grad_rows)
        *parts, du, u_sum[layer] = call(
            feed_back_body, half + [((RUN, 512), BF), ((1, 512), F32)], *g_rows, feed, u
        )
        if layer == 0:
            grad_att = finish_y(waiting, (256, ATT), after=(du,))
        blocks, added = scatter_rows(*parts)
        waiting = call(
            feed_grads_body, [((256, MLP), BF)] * 4, at, *g_rows, *b_rows, du, gelu_low,
            scalars=1, flops=4 * RUN * D * 512, after=(added,),
        )
        dh, dh_low, sums_two[layer] = call(
            mid_back_body,
            [((64, D), F32), ((64, D), BF), ((4, D), F32)],
            grad_rows, hidden, *blocks, par,
        )
        h_rows = gather_rows(dh_low)
        *parts, dqkv, qv_sum[layer] = call(
            attend_back_body,
            half + [((RUN, 384), BF), ((2, 128), F32)],
            *h_rows, att, mask, qkv, attended,
        )
        feed_sums[layer] = finish_y(waiting, (256, MLP), after=(dqkv,))
        if layer == 0:
            last = call(
                last_grads_body,
                [((288, ATT), BF)] * 4 + [((16, D), F32)],
                at, *a_rows, *h_rows, dqkv, att_low, *parts, pars[0],
                sums_two[0], sums_one[1], sums_two[1], qv_sum[0], u_sum[0], qv_sum[1], u_sum[1],
                scalars=1,
            )
        blocks, added = scatter_rows(*parts)
        if layer:
            waiting = call(
                attend_grads_body, [((256, ATT), BF)] * 4, at, *a_rows, *h_rows, dqkv, att_low,
                scalars=1, flops=2 * RUN * D * 512, after=(added,),
            )
        grad_rows, sums_one[layer] = call(
            end_back_body, [((64, D), BF), ((2, D), F32)], dh, rows, *blocks, par
        )
        inputs_back[layer] = grad_rows

    messages = last[:4]
    feed_out = call(
        feed_blocks_body, [((128, MLP), BF)] * 4, at, *feed_sums, scalars=1, after=(messages[0],)
    )
    feed_in = [feed_out[0]] + [x_shift(feed_out[j], -j) for j in (1, 2, 3)]
    att_in = [messages[0]] + [shift(messages[j], "y", -j) for j in (1, 2, 3)]
    att_out = call(attend_blocks_body, [((160, ATT), BF)] * 4, at, *att_in, grad_att, scalars=1)
    att_in = [att_out[0]] + [x_shift(att_out[j], -j) for j in (1, 2, 3)]
    *out, _ = call(
        z_blocks_body,
        [((48, 1536), BF)] * 4 + [((128, 1536), BF)],
        at, *att_in, *feed_in, scalars=1,
    )
    came = [out[0]] + [shift(out[j], "z", -j) for j in (1, 2, 3)]
    grad_qkv, grad_out, grad_up, grad_down, vector, side = call(
        finish_body,
        [((3, 32, 512), F32), ((32, 512), F32), ((32, 2048), F32), ((32, 2048), F32), ((6, D), F32), ((8, 128), F32)],
        at, *came, scalars=1,
    )
    vector = vector + swap(vector, "tensor")
    grad_qv = jnp.transpose(side[:4, :8].reshape(4, 2, 4), (1, 0, 2)).reshape(1, 2, 16, 1)
    grad_upb = side[:4, 8:24].reshape(1, 64, 1)

    def own_layer(per_layer):
        kept = jnp.where(section == 0, per_layer[0], per_layer[1])
        sent = swap(jnp.where(section == 0, per_layer[1], per_layer[0]), "section")
        return jnp.stack(
            [jnp.where(section == 0, kept, sent), jnp.where(section == 0, sent, kept)]
        )[None]

    return (
        own_layer(acts),
        own_layer(inputs_back),
        grad_qkv[None],
        grad_out.T[None],
        grad_up[None],
        grad_down.T[None],
        vector[None, 0:2],
        vector[None, 2:6],
        grad_qv,
        grad_upb,
    )


def solution(mesh):
    fine = Mesh(mesh.devices.reshape(2, 2, 4, 4, 2), ("section", "xh", "y", "z", "tensor"))
    dp = ("xh", "y", "z")
    return jax.shard_map(
        shards,
        mesh=fine,
        in_specs=(
            P(None, (*dp, "tensor"), None),
            P(None, (*dp, "tensor"), None),
            P(),
            P("section", None, dp, "tensor"),
            P("section", "tensor", dp),
            P("section", dp, "tensor"),
            P("section", "tensor", dp),
            P("section", None, None),
            P("section", None, None),
            P("section", None, "tensor", dp),
            P("section", "tensor", dp),
        ),
        out_specs=(
            P("section", None, (*dp, "tensor"), None),
            P("section", None, (*dp, "tensor"), None),
            P("section", None, dp, "tensor"),
            P("section", "tensor", dp),
            P("section", dp, "tensor"),
            P("section", "tensor", dp),
            P("section", None, None),
            P("section", None, None),
            P("section", None, "tensor", dp),
            P("section", "tensor", dp),
        ),
        check_vma=False,
    )
```

```python
import jax
import jax.numpy as jnp
from jax import lax
from jax.experimental import pallas as pl
from jax.experimental.pallas import tpu as pltpu
from jax.sharding import Mesh, PartitionSpec as P

D = 1024
HD = 64
VEC = 32
RUN = 512
EPS = 1e-05
MASKED = -1e30
BF = jnp.bfloat16
F32 = jnp.float32
ATT = 512
MLP = 1024
MIB = 1024 * 1024


def call(body, outs, *args, flops=0, scalars=0, after=(), vmem=16, scratch=(), outside=False):
    space = pltpu.HBM if outside else pltpu.VMEM
    specs = [pl.BlockSpec(memory_space=pltpu.SMEM)] * scalars
    specs += [pl.BlockSpec(memory_space=space)] * (len(args) - scalars)
    specs += [pl.BlockSpec(memory_space=pl.ANY)] * len(after)
    count = len(args)

    def kernel(*refs):
        body(*refs[:count], *refs[count + len(after) :])

    return pl.pallas_call(
        kernel,
        out_shape=[jax.ShapeDtypeStruct(shape, dtype) for shape, dtype in outs],
        in_specs=specs,
        out_specs=[pl.BlockSpec(memory_space=pltpu.VMEM)] * len(outs),
        scratch_shapes=list(scratch),
        compiler_params=pltpu.CompilerParams(vmem_limit_bytes=vmem * MIB),
        cost_estimate=pl.CostEstimate(
            flops=flops, bytes_accessed=MIB // 8, transcendentals=0
        ),
    )(*args, *after)


def dot(a, b, ca=1, cb=0):
    return lax.dot_general(a, b, (((ca,), (cb,)), ((), ())), preferred_element_type=F32)


def shift(array, axis, by, size=4):
    return lax.ppermute(array, axis, [((i + by) % size, i) for i in range(size)])


def x_shift(array, by):
    def rank(x):
        return (x % 2) * 2 + x // 2

    pairs = [(rank((x + by) % 4), rank(x)) for x in range(4)]
    return lax.ppermute(array, ("section", "xh"), pairs)


def flip(array):
    return lax.ppermute(array, "y", [(i, i ^ 1) for i in range(4)])


def mirror(array):
    return lax.ppermute(array, "y", [(i, 3 - i) for i in range(4)])


def swap(array, axis):
    return lax.ppermute(array, axis, [(0, 1), (1, 0)])


def gather_rows(rows):
    across, *sides = [shift(rows, "z", j) for j in (2, 1, 3)]
    mine = [rows, sides[0], across, sides[1]]
    return mine + [swap(piece, "tensor") for piece in mine]


def whole(refs, first=0):
    return jnp.concatenate([ref[first : first + 64, :] for ref in refs])


def add_body(mine_ref, other_ref, *outs):
    n = outs[0].shape[0]
    for j, out in enumerate(outs):
        rows = pl.ds(n * j, n)
        total = mine_ref[rows, :].astype(F32) + other_ref[rows, :].astype(F32)
        out[...] = total.astype(out.dtype)


def scatter_rows(mine, other, after=()):
    arrived = swap(other, "tensor")
    n = mine.shape[0] // 4
    blocks = call(
        add_body, [((n, D), F32)] + [((n, D), BF)] * 3, mine, arrived, after=after
    )
    return [blocks[0]] + [shift(blocks[j], "z", -j) for j in (2, 1, 3)], blocks[1]


def norm_stats(values):
    centred = values - jnp.mean(values, axis=-1, keepdims=True)
    rstd = lax.rsqrt(jnp.mean(centred * centred, axis=-1, keepdims=True) + EPS)
    return centred * rstd, rstd


def norm_back(grad, unit, rstd, gain):
    scaled = grad * gain
    return rstd * (
        scaled
        - jnp.mean(scaled, axis=-1, keepdims=True)
        - unit * jnp.mean(scaled * unit, axis=-1, keepdims=True)
    )


def total_of(refs):
    total = refs[0][...]
    for ref in refs[1:]:
        total = total + ref[...].astype(F32)
    return total


def first_norm_body(x_ref, g_ref, par_ref, out_ref):
    unit, _ = norm_stats(x_ref[...].astype(F32))
    par = par_ref[...].astype(F32)
    out_ref[:64, :] = (unit * par[0:1] + par[2:3]).astype(BF)
    out_ref[64:, :] = g_ref[...]


def mid_body(x_ref, b0, b1, b2, b3, par_ref, hidden_ref, out_ref):
    par = par_ref[...].astype(F32)
    hidden = x_ref[...].astype(F32) + total_of((b0, b1, b2, b3)) + par[4:5]
    hidden_ref[...] = hidden
    unit, _ = norm_stats(hidden)
    out_ref[...] = (unit * par[1:2] + par[3:4]).astype(BF)


def end_body(hidden_ref, b0, b1, b2, b3, par_ref, next_ref, act_ref, out_ref):
    par = par_ref[...].astype(F32)
    act = (hidden_ref[...] + total_of((b0, b1, b2, b3)) + par[5:6]).astype(BF)
    act_ref[...] = act
    unit, _ = norm_stats(act.astype(F32))
    later = next_ref[...].astype(F32)
    out_ref[...] = (unit * later[0:1] + later[2:3]).astype(BF)


def head_lanes(h):
    lane = lax.broadcasted_iota(jnp.int32, (1, 2 * HD), 1)
    return (lane >= h * HD) & (lane < (h + 1) * HD)


def column_bias(side_ref, first, count):
    side = side_ref[...].reshape(8, 16, 128)[:, :4].reshape(32, 128)
    n = 32 * count
    lane = lax.broadcasted_iota(jnp.int32, (128, n), 0)
    entry = lax.broadcasted_iota(jnp.int32, (128, n), 1)
    spread = dot(side, (lane == first + entry // 32).astype(F32))
    device = lax.broadcasted_iota(jnp.int32, (32, n), 0)
    entry = lax.broadcasted_iota(jnp.int32, (32, n), 1)
    return jnp.sum(jnp.where(entry % 32 == device, spread, 0.0), axis=0, keepdims=True)


def attend_body(*refs):
    rows = whole(refs[:8])
    w_ref, side_ref, mask_ref, out_mine, out_other, qkv_ref, att_ref, low_ref = refs[8:]
    projected = dot(rows, w_ref[:, : 3 * 128])
    q = (projected[:, :128] + column_bias(side_ref, 0, 4)).astype(BF)
    k = projected[:, 128:256].astype(BF)
    v = (projected[:, 256:] + column_bias(side_ref, 4, 4)).astype(BF)
    qkv_ref[0] = q
    qkv_ref[1] = k
    qkv_ref[2] = v
    zero = jnp.zeros((), BF)
    attended = jnp.zeros((RUN, 128), F32)
    for h in range(2):
        lanes = head_lanes(h)
        scores = dot(jnp.where(lanes, q, zero), k, 1, 1) * HD**-0.5 + mask_ref[...]
        weights = jnp.exp(scores - jnp.max(scores, axis=-1, keepdims=True))
        total = jnp.sum(weights, axis=-1, keepdims=True)
        attended += dot(weights.astype(BF), jnp.where(lanes, v, zero)) / total
    att_ref[...] = attended
    low = attended.astype(BF)
    low_ref[...] = low
    part = dot(low, w_ref[:, 384:512], 1, 1)
    out_mine[...] = part[:256].astype(BF)
    out_other[...] = part[256:].astype(BF)


def attend_back_body(*refs):
    rows = whole(refs[:8])
    w_ref, mask_ref, qkv_ref, att_ref, out_mine, out_other, grad_ref, sum_ref = refs[8:]
    grad_low = dot(rows, w_ref[:, 384:512]).astype(BF)
    grad_out = grad_low.astype(F32)
    q, k, v = qkv_ref[0], qkv_ref[1], qkv_ref[2]
    zero = jnp.zeros((), BF)
    products = grad_out * att_ref[...]
    dq = jnp.zeros((RUN, 128), F32)
    dk = jnp.zeros((RUN, 128), F32)
    dv = jnp.zeros((RUN, 128), F32)
    for h in range(2):
        lanes = head_lanes(h)
        q_h = jnp.where(lanes, q, zero)
        scores = dot(q_h, k, 1, 1) * HD**-0.5 + mask_ref[...]
        weights = jnp.exp(scores - jnp.max(scores, axis=-1, keepdims=True))
        inverse = 1.0 / jnp.sum(weights, axis=-1, keepdims=True)
        delta = jnp.sum(jnp.where(lanes, products, 0.0), axis=-1, keepdims=True)
        grad_h = jnp.where(lanes, grad_low, zero)
        grad_probs = dot(grad_h, v, 1, 1)
        grad_scores = (weights * inverse * (grad_probs - delta)).astype(BF)
        dq += dot(grad_scores, jnp.where(lanes, k, zero))
        dk += dot(grad_scores, q_h, 0, 0)
        scaled = (jnp.where(lanes, grad_out, 0.0) * inverse).astype(BF)
        dv += dot(weights.astype(BF), scaled, 0, 0)
    dq = (dq * HD**-0.5).astype(BF)
    dk = (dk * HD**-0.5).astype(BF)
    dv = dv.astype(BF)
    grads = jnp.concatenate([dq, dk, dv], axis=1)
    grad_ref[...] = grads
    sum_ref[0:1, :] = jnp.sum(dq.astype(F32), axis=0, keepdims=True)
    sum_ref[1:2, :] = jnp.sum(dv.astype(F32), axis=0, keepdims=True)
    part = dot(grads, w_ref[:, : 3 * 128], 1, 1)
    out_mine[...] = part[:256].astype(BF)
    out_other[...] = part[256:].astype(BF)


def gelu_parts(u):
    cubic = 0.044715 * u * u
    t = jnp.tanh(0.7978845608028654 * u * (1.0 + cubic))
    return t, cubic


def feed_body(*refs):
    rows = whole(refs[:8])
    w_ref, side_ref, out_mine, out_other, u_ref, z_ref = refs[8:]
    u = dot(rows, w_ref[:, :512]) + column_bias(side_ref, 8, 16)
    u_ref[...] = u
    t, _ = gelu_parts(u)
    z = (0.5 * u * (1.0 + t)).astype(BF)
    z_ref[...] = z
    part = dot(z, w_ref[:, 512:], 1, 1)
    out_mine[...] = part[:256].astype(BF)
    out_other[...] = part[256:].astype(BF)


def feed_back(grad_z, u):
    t, cubic = gelu_parts(u)
    slope = 0.5 * (1.0 + t) + 0.5 * u * (1.0 - t * t) * 0.7978845608028654 * (1.0 + 3.0 * cubic)
    return (grad_z * slope).astype(BF)


def feed_back_body(*refs):
    rows = whole(refs[:8])
    w_ref, u_ref, out_mine, out_other, du_ref, sum_ref = refs[8:]
    du = feed_back(dot(rows, w_ref[:, 512:]), u_ref[...])
    du_ref[...] = du
    sum_ref[...] = jnp.sum(du.astype(F32), axis=0, keepdims=True)
    part = dot(du, w_ref[:, :512], 1, 1)
    out_mine[...] = part[:256].astype(BF)
    out_other[...] = part[256:].astype(BF)


def feed_turn_body(*refs):
    rows, grad_rows = whole(refs[:8]), whole(refs[8:16], 64)
    w_ref, side_ref, out_mine, out_other, z_ref, du_ref, sum_ref = refs[16:]
    u = dot(rows, w_ref[:, :512]) + column_bias(side_ref, 8, 16)
    t, _ = gelu_parts(u)
    z = (0.5 * u * (1.0 + t)).astype(BF)
    z_ref[...] = z
    du = feed_back(dot(grad_rows, w_ref[:, 512:]), u)
    du_ref[...] = du
    sum_ref[...] = jnp.sum(du.astype(F32), axis=0, keepdims=True)
    for first, part in ((0, dot(z, w_ref[:, 512:], 1, 1)), (64, dot(du, w_ref[:, :512], 1, 1))):
        for j in range(4):
            rows = slice(128 * j + first, 128 * j + first + 64)
            out_mine[rows, :] = part[64 * j : 64 * j + 64].astype(BF)
            out_other[rows, :] = part[256 + 64 * j : 320 + 64 * j].astype(BF)


def mid_back(g, hidden, grad, par, dh_ref, low_ref, sums_ref):
    unit, rstd = norm_stats(hidden)
    dh = g + norm_back(grad, unit, rstd, par[1:2])
    low = dh.astype(BF)
    dh_ref[...] = dh
    low_ref[...] = low
    sums_ref[0:1, :] = jnp.sum(grad * unit, axis=0, keepdims=True)
    sums_ref[1:2, :] = jnp.sum(grad, axis=0, keepdims=True)
    sums_ref[2:3, :] = jnp.sum(low.astype(F32), axis=0, keepdims=True)
    sums_ref[3:4, :] = jnp.sum(g, axis=0, keepdims=True)


def mid_back_body(g_ref, hidden_ref, b0, b1, b2, b3, par_ref, dh_ref, low_ref, sums_ref):
    grad = total_of((b0, b1, b2, b3))
    mid_back(
        g_ref[...].astype(F32), hidden_ref[...], grad, par_ref[...].astype(F32), dh_ref, low_ref, sums_ref
    )


def turn_body(g_ref, hidden_ref, b0, b1, b2, b3, par_ref, act_ref, dh_ref, low_ref, sums_ref):
    total = total_of((b0, b1, b2, b3))
    par = par_ref[...].astype(F32)
    hidden = hidden_ref[...]
    act_ref[...] = (hidden + total[:64] + par[5:6]).astype(BF)
    mid_back(g_ref[...].astype(F32), hidden, total[64:], par, dh_ref, low_ref, sums_ref)


def end_back_body(dh_ref, x_ref, b0, b1, b2, b3, par_ref, out_ref, sums_ref):
    par = par_ref[...].astype(F32)
    grad = total_of((b0, b1, b2, b3))
    unit, rstd = norm_stats(x_ref[...].astype(F32))
    out_ref[...] = (dh_ref[...] + norm_back(grad, unit, rstd, par[0:1])).astype(BF)
    sums_ref[0:1, :] = jnp.sum(grad * unit, axis=0, keepdims=True)
    sums_ref[1:2, :] = jnp.sum(grad, axis=0, keepdims=True)


def feed_grads_body(*refs):
    g, b = whole(refs[:8]), whole(refs[8:16])
    du_ref, z_ref, out_ref = refs[16:]
    out_ref[:, :512] = dot(b, du_ref[...], 0, 0).astype(BF)
    out_ref[:, 512:] = dot(g, z_ref[...], 0, 0).astype(BF)


def other_places(y):
    flipped = y + 1 - 2 * lax.rem(y, 2)
    return flipped, 3 - y, 3 - flipped


def halving_messages(at_ref, full, keep, send):
    y = at_ref[3]
    flipped, mirrored, across = other_places(y)
    for half in range(2):
        rows = slice(128 * half, 128 * half + 128)
        for out, i, place in ((keep, 0, y), (keep, 1, mirrored), (send, 0, flipped), (send, 1, across)):
            out[i, rows, :] = full[pl.ds(pl.multiple_of((half * 4 + place) * 128, 128), 128), :]


def feed_grads(first, at_ref, refs):
    g, b = whole(refs[:8], first), whole(refs[8:16])
    du_ref, z_ref, *outs, full = refs[16:]
    full[:, :512] = dot(b, du_ref[...], 0, 0).astype(BF)
    full[:, 512:] = dot(g, z_ref[...], 0, 0).astype(BF)
    halving_messages(at_ref, full, *outs)


def attend_grads(refs, full):
    a, h = whole(refs[:8]), whole(refs[8:16])
    dqkv_ref, low_ref = refs[16:18]
    full[:, :384] = dot(a, dqkv_ref[...], 0, 0).astype(BF)
    full[:, 384:] = dot(h, low_ref[...], 0, 0).astype(BF)
    return a


def attend_grads_body(at_ref, *refs):
    attend_grads(refs, refs[-1])
    halving_messages(at_ref, refs[-1], *refs[18:20])


def halve_body(keep, came, mine, later):
    mine[...] = keep[0].astype(F32) + came[0].astype(F32)
    later[...] = (keep[1].astype(F32) + came[1].astype(F32)).astype(BF)


def halve_end_body(mine, came, out):
    out[...] = (mine[...] + came[...].astype(F32)).astype(BF)


def pack_body(at_ref, qkv_hbm, out_hbm, up_hbm, down_hbm, qv_hbm, upb_hbm, *refs):
    outs, held, sems = refs[:4], refs[4:10], refs[10]
    copies = [
        pltpu.make_async_copy(source, to, sems.at[i])
        for i, (source, to) in enumerate(
            zip((qkv_hbm, out_hbm, up_hbm, down_hbm, qv_hbm, upb_hbm), held)
        )
    ]
    for copy in copies:
        copy.start()
    for copy in copies:
        copy.wait()
    qkv_ref, out_ref, up_ref, down_ref, qv_ref, upb_ref = held
    qv = qv_ref[...].astype(F32)
    upb = upb_ref[...].astype(F32)

    def pick(row, first, count, start):
        n = row.shape[1]
        entry = lax.broadcasted_iota(jnp.int32, (n, 128), 0)
        lane = lax.broadcasted_iota(jnp.int32, (n, 128), 1)
        chosen = (entry == start + lane - first) & (lane >= first) & (lane < first + count)
        return dot(jnp.broadcast_to(row, (16, n)), chosen.astype(F32))

    for j in range(4):
        to = lax.rem(at_ref[0] + j, 4)
        narrow = pl.ds(pl.multiple_of(to * 128, 128), 128)
        broad = pl.ds(pl.multiple_of(to * 512, 512), 512)
        att = outs[j]
        for i in range(3):
            att[:32, 128 * i : 128 * i + 128] = qkv_ref[i, :, narrow]
        att[:32, 384:] = out_ref[:, narrow]
        side = pick(qv[0:1], 0, 4, 4 * to) + pick(qv[1:2], 4, 4, 4 * to) + pick(upb, 8, 16, 16 * to)
        att[32:48, :128] = side.astype(BF)
        att[32:48, 128:] = jnp.zeros((16, 384), BF)
        att[48:80, :] = up_ref[:, broad]
        att[80:, :] = down_ref[:, broad]


def collect_body(at_ref, *refs):
    att_ref, feed_ref = refs[4:]
    row = lax.broadcasted_iota(jnp.int32, (16, 512), 0)
    side = jnp.zeros((16, 512), F32)
    for j in range(4):
        place = lax.rem(at_ref[0] + 4 - j, 4)
        rows = pl.ds(pl.multiple_of(place * 32, 32), 32)
        att_ref[rows, :] = refs[j][:32, :]
        feed_ref[rows, :512] = refs[j][48:80, :]
        feed_ref[rows, 512:] = refs[j][80:, :]
        side = jnp.where(row == place, refs[j][32:48, :].astype(F32), side)
    att_ref[128:, :] = side.astype(BF)


def select_body(layer, at_ref, own, right, left, across, out):
    section, xh = at_ref[1], at_ref[2]
    out[xh] = jnp.where(section == layer, own[...], (right if layer else left)[...])
    out[1 - xh] = jnp.where(section == layer, across[...], (left if layer else right)[...])


def place_y_body(at_ref, *refs):
    for j in range(4):
        place = lax.rem(at_ref[3] + j, 4)
        for half in range(2):
            rows = pl.ds(pl.multiple_of((half * 4 + place) * 128, 128), 128)
            refs[4][rows, :] = refs[j][half, :128, :]
            if len(refs) > 5:
                rows = pl.ds(pl.multiple_of((half * 4 + place) * 16, 16), 16)
                refs[5][rows, :] = refs[j][half, 128:, :128]


def last_grads_body(at_ref, *refs):
    mine, other, par_ref, two0, one1, two1, qv0, u0, qv1, u1 = refs[18:28]
    outs, (sums, full) = refs[28:32], refs[32:]
    a = attend_grads(refs, full)
    par = par_ref[...].astype(F32)
    part = jnp.concatenate([mine[...], other[...]]).astype(F32)
    unit = (a.astype(F32) - par[2:3]) / par[0:1]
    sums[...] = jnp.zeros((16, D), F32)
    sums[0:1, :] = jnp.sum(part * unit, axis=0, keepdims=True)
    sums[1:2, :] = two0[0:1, :]
    sums[2:3, :] = jnp.sum(part, axis=0, keepdims=True)
    sums[3:6, :] = two0[1:4, :]
    sums[6:7, :] = one1[0:1, :]
    sums[7:8, :] = two1[0:1, :]
    sums[8:9, :] = one1[1:2, :]
    sums[9:12, :] = two1[1:4, :]
    for row, qv, u in ((12, qv0, u0), (13, qv1, u1)):
        sums[row : row + 1, :128] = qv[0:1, :]
        sums[row : row + 1, 128:256] = qv[1:2, :]
        sums[row : row + 1, 256:768] = u[...]
    low = sums[...].astype(BF)
    for j, out in enumerate(outs):
        place = lax.rem(at_ref[3] + j, 4)
        for half in range(2):
            rows = pl.ds(pl.multiple_of((half * 4 + place) * 128, 128), 128)
            out[128 * half : 128 * half + 128, :] = full[rows, :]
        out[256:272, :] = low[:, :512]
        out[272:288, :] = low[:, 512:]


def sum_of(refs):
    total = refs[0][...].astype(F32)
    for ref in refs[1:]:
        total = total + ref[...].astype(F32)
    return total


def target_x(at_ref, j):
    x = lax.rem(at_ref[2] * 2 + at_ref[1] + j, 4)
    return lax.rem(x, 2), x // 2


def feed_blocks_body(at_ref, first, second, *outs):
    for j, out in enumerate(outs):
        layer, half = target_x(at_ref, j)
        rows = pl.ds(pl.multiple_of(half * 128, 128), 128)
        out[...] = jnp.where(layer == 0, first[rows, :], second[rows, :])


def attend_blocks_body(at_ref, m0, m1, m2, m3, second, *outs):
    total = sum_of((m0, m1, m2, m3))
    low = total.astype(BF)
    for j, out in enumerate(outs):
        layer, half = target_x(at_ref, j)
        own = jnp.where(half == 0, low[:128], low[128:256])
        rows = pl.ds(pl.multiple_of(half * 128, 128), 128)
        out[:128, :] = jnp.where(layer == 0, own, second[rows, :])
        out[128:, :] = low[256:]


def z_blocks_body(at_ref, a0, a1, a2, a3, f0, f1, f2, f3, o0, o1, o2, o3, rows_ref):
    att = sum_of((a0, a1, a2, a3)).astype(BF)
    rows_ref[:, :512] = att[:128]
    rows_ref[:, 512:] = sum_of((f0, f1, f2, f3)).astype(BF)
    for j, out in enumerate((o0, o1, o2, o3)):
        to = lax.rem(at_ref[0] + j, 4)
        out[:32, :] = rows_ref[pl.ds(pl.multiple_of(to * 32, 32), 32), :]
        out[32:, :512] = att[128:144]
        out[32:, 512:1024] = att[144:160]
        out[32:, 1024:] = jnp.zeros((16, 512), BF)


def finish_body(at_ref, m0, m1, m2, m3, qkv_ref, out_ref, up_ref, down_ref, vector_ref, side_ref):
    row = lax.broadcasted_iota(jnp.int32, (8, 768), 0)
    total = jnp.zeros((16, D), F32)
    side = jnp.zeros((8, 768), F32)
    section = at_ref[1]
    for j, ref in enumerate((m0, m1, m2, m3)):
        place = lax.rem(at_ref[0] + 4 - j, 4)
        narrow = pl.ds(pl.multiple_of(place * 128, 128), 128)
        broad = pl.ds(pl.multiple_of(place * 512, 512), 512)
        for i in range(3):
            qkv_ref[i, :, narrow] = ref[:32, 128 * i : 128 * i + 128].astype(F32)
        out_ref[:, narrow] = ref[:32, 384:512].astype(F32)
        up_ref[:, broad] = ref[:32, 512:1024].astype(F32)
        down_ref[:, broad] = ref[:32, 1024:].astype(F32)
        sums = ref[32:, :1024].astype(F32)
        total = total + sums
        own = jnp.where(section == 0, sums[12:13, :768], sums[13:14, :768])
        side = jnp.where(row == place, own, side)
    vector_ref[...] = jnp.where(section == 0, total[:6], total[6:12])
    index = (at_ref[2] * 4 + at_ref[3]) * 4 + at_ref[0]
    entry = lax.broadcasted_iota(jnp.int32, (8, 768), 1)
    kept = jnp.where(entry % 32 == index, side, 0.0)
    entry = lax.broadcasted_iota(jnp.int32, (768, 128), 0)
    lane = lax.broadcasted_iota(jnp.int32, (768, 128), 1)
    side_ref[...] = dot(kept, (entry // 32 == lane).astype(F32))


def shards(inputs, cotangent, segments, qkv_weight, out_weight, up_weight, down_weight, norm_gains, biases, qv_bias, up_bias):
    section, xh, y, z = (lax.axis_index(name) for name in ("section", "xh", "y", "z"))
    core = lax.axis_index("tensor")
    at = jnp.stack([z, section, xh, y]).astype(jnp.int32)
    x0 = lax.dynamic_index_in_dim(inputs, section, 0, keepdims=False)
    g1 = lax.dynamic_index_in_dim(cotangent, section, 0, keepdims=False)
    own_par = jnp.concatenate([norm_gains[0], biases[0]])
    other_par = swap(own_par, "section")

    sources = (
        qkv_weight[0], out_weight[0].T, up_weight[0], down_weight[0].T, qv_bias[0, :, :, 0], up_bias[0].T
    )
    packed = call(
        pack_body,
        [((112, ATT), BF)] * 4,
        at, *sources,
        scalars=1,
        outside=True,
        vmem=56,
        scratch=[pltpu.VMEM(a.shape, BF) for a in sources] + [pltpu.SemaphoreType.DMA((6,))],
    )
    came = [packed[0]] + [shift(packed[j], "z", -j) for j in (1, 2, 3)]
    att_rows, feed_rows = call(
        collect_body, [((144, ATT), BF), ((128, MLP), BF)], at, *came, scalars=1
    )

    def along_x(part):
        return [part] + [x_shift(part, j) for j in (1, 3, 2)]

    def along_y(layer, pieces, after=()):
        body = lambda *refs: select_body(layer, *refs)
        (rows,) = call(
            body, [((2, *pieces[0].shape), BF)], at, *pieces, scalars=1, after=after
        )
        return [rows] + [shift(rows, "y", j) for j in (1, 2, 3)]

    att_outs = [((D, ATT), BF), ((128, 128), BF)]
    feed_outs = [((D, MLP), BF)]
    att_x = along_x(att_rows)
    att_y = along_y(0, att_x)
    feed_x = along_x(feed_rows)

    row = lax.dynamic_index_in_dim(segments, section, 0, keepdims=False)
    run = lax.dynamic_slice_in_dim(row, (xh * 4 + y) * RUN, RUN)
    marks = jnp.stack([jnp.arange(RUN, dtype=jnp.int32), run]).reshape(2, 4, 2, 64)
    marks = lax.dynamic_slice_in_dim(jnp.concatenate([marks, marks], axis=1), z, 4, 1)
    marks = jnp.where(core == 0, marks, marks[:, :, ::-1])
    marks = jnp.transpose(marks, (0, 2, 1, 3)).reshape(2, RUN)
    allowed = (marks[0][None, :] <= marks[0][:, None]) & (marks[1][None, :] == marks[1][:, None])
    mask = jnp.where(allowed, 0.0, MASKED).astype(F32)

    pars = [
        jnp.where(section == 0, own_par, other_par),
        jnp.where(section == 0, other_par, own_par),
    ]

    half = [((256, D), BF)] * 2
    saved = []
    acts = [None, None]
    weights = []
    rows = x0
    normed = call(first_norm_body, [((128, D), BF)], x0, g1, pars[0])[0]
    for layer in (0, 1):
        par = pars[layer]
        a_rows = gather_rows(normed)
        if layer == 0:
            g_rows = a_rows
            att, side = call(
                place_y_body, att_outs, at, *att_y, scalars=1, after=[*a_rows, mask]
            )
        else:
            att, side = call(
                place_y_body, att_outs, at, *att_y, scalars=1, after=a_rows[:4]
            )
        feed_y = along_y(layer, feed_x, after=(att,))
        *parts, qkv, attended, att_low = call(
            attend_body,
            half + [((3, RUN, 128), BF), ((RUN, 128), F32), ((RUN, 128), BF)],
            *a_rows, att, side, mask, after=(feed_y[0],),
        )
        blocks, added = scatter_rows(*parts)
        hidden, second = call(
            mid_body, [((64, D), F32), ((64, D), BF)], rows, *blocks, par
        )
        b_rows = gather_rows(second)
        (feed,) = call(place_y_body, feed_outs, at, *feed_y, scalars=1, after=b_rows[:4])
        weights.append((att, feed))
        if layer == 0:
            att_y = along_y(1, att_x, after=(feed,))
            *parts, u, gelu_low = call(
                feed_body,
                half + [((RUN, 512), F32), ((RUN, 512), BF)],
                *b_rows, feed, side, after=(att_y[0],),
            )
            blocks, added = scatter_rows(*parts)
            saved.append((rows, a_rows, qkv, attended, att_low, hidden, b_rows, u, gelu_low))
            rows, normed = call(
                end_body, [((64, D), BF)] * 2, hidden, *blocks, par, pars[1]
            )
            acts[0] = rows

    inputs_back = [None, None]
    sums_two = [None, None]
    sums_one = [None, None]
    u_sum = [None, None]
    qv_sum = [None, None]
    feed_sums = [None, None]
    grad_rows = g1

    def halve(messages, after):
        keep, send = messages
        shape = keep.shape[1:]
        mine, later = call(halve_body, [(shape, F32), (shape, BF)], keep, flip(send), after=after)
        return mine, mirror(later)

    def halve_end(pieces, after):
        return call(halve_end_body, [(pieces[0].shape, BF)], *pieces, after=after)[0]

    def message_shapes(n):
        return [((2, 256, n), BF)] * 2

    for layer in (1, 0):
        att, feed = weights[layer]
        par = pars[layer]
        if layer:
            *parts, gelu_low, du, u_sum[1] = call(
                feed_turn_body,
                [((512, D), BF)] * 2 + [((RUN, 512), BF)] * 2 + [((1, 512), F32)],
                *b_rows, *g_rows, feed, side,
            )
            blocks, added = scatter_rows(*parts)
            order = (added,)
        else:
            rows, a_rows, qkv, attended, att_low, hidden, b_rows, u, gelu_low = saved[0]
            g_rows = gather_rows(grad_rows)
            att_step = halve(att_messages, after=())
            *parts, du, u_sum[0] = call(
                feed_back_body, half + [((RUN, 512), BF), ((1, 512), F32)], *g_rows, feed, u,
                after=(feed_sums[1], att_step[0]),
            )
            blocks, added = scatter_rows(*parts)
            grad_att = halve_end(att_step, after=(added,))
            order = (added,)
        body = lambda at_ref, *refs, first=64 * layer: feed_grads(first, at_ref, refs)
        messages = call(
            body, message_shapes(MLP), at, *g_rows, *b_rows, du, gelu_low,
            scalars=1, flops=4 * RUN * D * 512, after=order, scratch=[pltpu.VMEM((D, MLP), BF)],
        )
        if layer:
            acts[1], dh, dh_low, sums_two[1] = call(
                turn_body,
                [((64, D), BF), ((64, D), F32), ((64, D), BF), ((4, D), F32)],
                grad_rows, hidden, *blocks, par, after=(messages[0],),
            )
        else:
            dh, dh_low, sums_two[0] = call(
                mid_back_body,
                [((64, D), F32), ((64, D), BF), ((4, D), F32)],
                grad_rows, hidden, *blocks, par, after=(messages[0],),
            )
        h_rows = gather_rows(dh_low)
        *parts, dqkv, qv_sum[layer] = call(
            attend_back_body,
            half + [((RUN, 384), BF), ((2, 128), F32)],
            *h_rows, att, mask, qkv, attended, after=() if layer else (grad_att,),
        )
        feed_step = halve(messages, after=(dqkv,))
        if layer == 0:
            last = call(
                last_grads_body,
                [((288, ATT), BF)] * 4,
                at, *a_rows, *h_rows, dqkv, att_low, *parts, pars[0],
                sums_two[0], sums_one[1], sums_two[1], qv_sum[0], u_sum[0], qv_sum[1], u_sum[1],
                scalars=1, after=(feed_step[0],), scratch=[pltpu.VMEM((16, D), F32), pltpu.VMEM((D, ATT), BF)],
            )
        blocks, added = scatter_rows(*parts, after=(feed_step[0],) if layer else ())
        feed_sums[layer] = halve_end(feed_step, after=(added,) if layer else (last[0],))
        if layer:
            att_messages = call(
                attend_grads_body, message_shapes(ATT), at, *a_rows, *h_rows, dqkv, att_low,
                scalars=1, flops=2 * RUN * D * 512, after=(added,),
                scratch=[pltpu.VMEM((D, ATT), BF)],
            )
        grad_rows, sums_one[layer] = call(
            end_back_body, [((64, D), BF), ((2, D), F32)], dh, rows, *blocks, par,
            after=(att_messages[0],) if layer else (),
        )
        inputs_back[layer] = grad_rows

    messages = last[:4]
    feed_out = call(
        feed_blocks_body, [((128, MLP), BF)] * 4, at, *feed_sums, scalars=1, after=(messages[0],)
    )
    feed_in = [feed_out[0]] + [x_shift(feed_out[j], -j) for j in (1, 2, 3)]
    att_in = [messages[0]] + [shift(messages[j], "y", -j) for j in (1, 2, 3)]
    att_out = call(attend_blocks_body, [((160, ATT), BF)] * 4, at, *att_in, grad_att, scalars=1)
    att_in = [att_out[0]] + [x_shift(att_out[j], -j) for j in (1, 2, 3)]
    *out, _ = call(
        z_blocks_body,
        [((48, 1536), BF)] * 4 + [((128, 1536), BF)],
        at, *att_in, *feed_in, scalars=1, after=(grad_rows,),
    )
    came = [out[0]] + [shift(out[j], "z", -j) for j in (1, 2, 3)]
    grad_qkv, grad_out, grad_up, grad_down, vector, side = call(
        finish_body,
        [((3, 32, 512), F32), ((32, 512), F32), ((32, 2048), F32), ((32, 2048), F32), ((6, D), F32), ((8, 128), F32)],
        at, *came, scalars=1,
    )
    vector = vector + swap(vector, "tensor")
    grad_qv = jnp.transpose(side[:4, :8].reshape(4, 2, 4), (1, 0, 2)).reshape(1, 2, 16, 1)
    grad_upb = side[:4, 8:24].reshape(1, 64, 1)

    def own_layer(per_layer):
        kept = jnp.where(section == 0, per_layer[0], per_layer[1])
        sent = swap(jnp.where(section == 0, per_layer[1], per_layer[0]), "section")
        return jnp.stack(
            [jnp.where(section == 0, kept, sent), jnp.where(section == 0, sent, kept)]
        )[None]

    return (
        own_layer(acts),
        own_layer(inputs_back),
        grad_qkv[None],
        grad_out.T[None],
        grad_up[None],
        grad_down.T[None],
        vector[None, 0:2],
        vector[None, 2:6],
        grad_qv,
        grad_upb,
    )


def solution(mesh):
    fine = Mesh(mesh.devices.reshape(2, 2, 4, 4, 2), ("section", "xh", "y", "z", "tensor"))
    dp = ("xh", "y", "z")
    return jax.shard_map(
        shards,
        mesh=fine,
        in_specs=(
            P(None, (*dp, "tensor"), None),
            P(None, (*dp, "tensor"), None),
            P(),
            P("section", None, dp, "tensor"),
            P("section", "tensor", dp),
            P("section", dp, "tensor"),
            P("section", "tensor", dp),
            P("section", None, None),
            P("section", None, None),
            P("section", None, "tensor", dp),
            P("section", "tensor", dp),
        ),
        out_specs=(
            P("section", None, (*dp, "tensor"), None),
            P("section", None, (*dp, "tensor"), None),
            P("section", None, dp, "tensor"),
            P("section", "tensor", dp),
            P("section", dp, "tensor"),
            P("section", "tensor", dp),
            P("section", None, None),
            P("section", None, None),
            P("section", None, "tensor", dp),
            P("section", "tensor", dp),
        ),
        check_vma=False,
    )
```

```python
import jax
import jax.numpy as jnp
from jax import lax
from jax.experimental import pallas as pl
from jax.experimental.pallas import tpu as pltpu
from jax.sharding import Mesh, PartitionSpec as P

D = 1024
HD = 64
VEC = 32
RUN = 512
EPS = 1e-05
MASKED = -1e30
BF = jnp.bfloat16
F32 = jnp.float32
ATT = 512
MLP = 1024
MIB = 1024 * 1024


def call(body, outs, *args, flops=0, scalars=0, after=(), vmem=16, scratch=(), outside=False):
    space = pltpu.HBM if outside else pltpu.VMEM
    specs = [pl.BlockSpec(memory_space=pltpu.SMEM)] * scalars
    specs += [pl.BlockSpec(memory_space=space)] * (len(args) - scalars)
    specs += [pl.BlockSpec(memory_space=pl.ANY)] * len(after)
    count = len(args)

    def kernel(*refs):
        body(*refs[:count], *refs[count + len(after) :])

    return pl.pallas_call(
        kernel,
        out_shape=[jax.ShapeDtypeStruct(shape, dtype) for shape, dtype in outs],
        in_specs=specs,
        out_specs=[pl.BlockSpec(memory_space=pltpu.VMEM)] * len(outs),
        scratch_shapes=list(scratch),
        compiler_params=pltpu.CompilerParams(vmem_limit_bytes=vmem * MIB),
        cost_estimate=pl.CostEstimate(
            flops=flops, bytes_accessed=MIB // 8, transcendentals=0
        ),
    )(*args, *after)


def dot(a, b, ca=1, cb=0):
    return lax.dot_general(a, b, (((ca,), (cb,)), ((), ())), preferred_element_type=F32)


def shift(array, axis, by, size=4):
    return lax.ppermute(array, axis, [((i + by) % size, i) for i in range(size)])


def x_shift(array, by):
    def rank(x):
        return (x % 2) * 2 + x // 2

    pairs = [(rank((x + by) % 4), rank(x)) for x in range(4)]
    return lax.ppermute(array, ("section", "xh"), pairs)


def flip(array):
    return lax.ppermute(array, "y", [(i, i ^ 1) for i in range(4)])


def mirror(array):
    return lax.ppermute(array, "y", [(i, 3 - i) for i in range(4)])


def swap(array, axis):
    return lax.ppermute(array, axis, [(0, 1), (1, 0)])


def gather_rows(rows):
    across, *sides = [shift(rows, "z", j) for j in (2, 1, 3)]
    mine = [rows, sides[0], across, sides[1]]
    return mine + [swap(piece, "tensor") for piece in mine]


def whole(refs, first=0):
    return jnp.concatenate([ref[first : first + 64, :] for ref in refs])


def add_body(mine_ref, other_ref, *outs):
    n = outs[0].shape[0]
    for j, out in enumerate(outs):
        rows = pl.ds(n * j, n)
        total = mine_ref[rows, :].astype(F32) + other_ref[rows, :].astype(F32)
        out[...] = total.astype(out.dtype)


def scatter_rows(mine, other, after=()):
    arrived = swap(other, "tensor")
    n = mine.shape[0] // 4
    blocks = call(
        add_body, [((n, D), F32)] + [((n, D), BF)] * 3, mine, arrived, after=after
    )
    return [blocks[0]] + [shift(blocks[j], "z", -j) for j in (2, 1, 3)], blocks[1]


def norm_stats(values):
    centred = values - jnp.mean(values, axis=-1, keepdims=True)
    rstd = lax.rsqrt(jnp.mean(centred * centred, axis=-1, keepdims=True) + EPS)
    return centred * rstd, rstd


def norm_back(grad, unit, rstd, gain):
    scaled = grad * gain
    return rstd * (
        scaled
        - jnp.mean(scaled, axis=-1, keepdims=True)
        - unit * jnp.mean(scaled * unit, axis=-1, keepdims=True)
    )


def total_of(refs):
    total = refs[0][...]
    for ref in refs[1:]:
        total = total + ref[...].astype(F32)
    return total


def first_norm_body(x_ref, g_ref, par_ref, out_ref):
    unit, _ = norm_stats(x_ref[...].astype(F32))
    par = par_ref[...].astype(F32)
    out_ref[:64, :] = (unit * par[0:1] + par[2:3]).astype(BF)
    out_ref[64:, :] = g_ref[...]


def mid_body(x_ref, b0, b1, b2, b3, par_ref, hidden_ref, out_ref):
    par = par_ref[...].astype(F32)
    hidden = x_ref[...].astype(F32) + total_of((b0, b1, b2, b3)) + par[4:5]
    hidden_ref[...] = hidden
    unit, _ = norm_stats(hidden)
    out_ref[...] = (unit * par[1:2] + par[3:4]).astype(BF)


def end_body(hidden_ref, b0, b1, b2, b3, par_ref, next_ref, act_ref, out_ref):
    par = par_ref[...].astype(F32)
    act = (hidden_ref[...] + total_of((b0, b1, b2, b3)) + par[5:6]).astype(BF)
    act_ref[...] = act
    unit, _ = norm_stats(act.astype(F32))
    later = next_ref[...].astype(F32)
    out_ref[...] = (unit * later[0:1] + later[2:3]).astype(BF)


def head_lanes(h):
    lane = lax.broadcasted_iota(jnp.int32, (1, 2 * HD), 1)
    return (lane >= h * HD) & (lane < (h + 1) * HD)


def column_bias(side_ref, first, count):
    side = side_ref[...].reshape(8, 16, 128)[:, :4].reshape(32, 128)
    n = 32 * count
    lane = lax.broadcasted_iota(jnp.int32, (128, n), 0)
    entry = lax.broadcasted_iota(jnp.int32, (128, n), 1)
    spread = dot(side, (lane == first + entry // 32).astype(F32))
    device = lax.broadcasted_iota(jnp.int32, (32, n), 0)
    entry = lax.broadcasted_iota(jnp.int32, (32, n), 1)
    return jnp.sum(jnp.where(entry % 32 == device, spread, 0.0), axis=0, keepdims=True)


def attend_body(*refs):
    rows = whole(refs[:8])
    w_ref, side_ref, mask_ref, out_mine, out_other, qkv_ref, att_ref, low_ref = refs[8:]
    projected = dot(rows, w_ref[:, : 3 * 128])
    q = (projected[:, :128] + column_bias(side_ref, 0, 4)).astype(BF)
    k = projected[:, 128:256].astype(BF)
    v = (projected[:, 256:] + column_bias(side_ref, 4, 4)).astype(BF)
    qkv_ref[0] = q
    qkv_ref[1] = k
    qkv_ref[2] = v
    zero = jnp.zeros((), BF)
    attended = jnp.zeros((RUN, 128), F32)
    for h in range(2):
        lanes = head_lanes(h)
        scores = dot(jnp.where(lanes, q, zero), k, 1, 1) * HD**-0.5 + mask_ref[...]
        weights = jnp.exp(scores - jnp.max(scores, axis=-1, keepdims=True))
        total = jnp.sum(weights, axis=-1, keepdims=True)
        attended += dot(weights.astype(BF), jnp.where(lanes, v, zero)) / total
    att_ref[...] = attended
    low = attended.astype(BF)
    low_ref[...] = low
    part = dot(low, w_ref[:, 384:512], 1, 1)
    out_mine[...] = part[:256].astype(BF)
    out_other[...] = part[256:].astype(BF)


def attend_back_body(*refs):
    rows = whole(refs[:8])
    w_ref, mask_ref, qkv_ref, att_ref, out_mine, out_other, grad_ref, sum_ref = refs[8:]
    grad_low = dot(rows, w_ref[:, 384:512]).astype(BF)
    grad_out = grad_low.astype(F32)
    q, k, v = qkv_ref[0], qkv_ref[1], qkv_ref[2]
    zero = jnp.zeros((), BF)
    products = grad_out * att_ref[...]
    dq = jnp.zeros((RUN, 128), F32)
    dk = jnp.zeros((RUN, 128), F32)
    dv = jnp.zeros((RUN, 128), F32)
    for h in range(2):
        lanes = head_lanes(h)
        q_h = jnp.where(lanes, q, zero)
        scores = dot(q_h, k, 1, 1) * HD**-0.5 + mask_ref[...]
        weights = jnp.exp(scores - jnp.max(scores, axis=-1, keepdims=True))
        inverse = 1.0 / jnp.sum(weights, axis=-1, keepdims=True)
        delta = jnp.sum(jnp.where(lanes, products, 0.0), axis=-1, keepdims=True)
        grad_h = jnp.where(lanes, grad_low, zero)
        grad_probs = dot(grad_h, v, 1, 1)
        grad_scores = (weights * inverse * (grad_probs - delta)).astype(BF)
        dq += dot(grad_scores, jnp.where(lanes, k, zero))
        dk += dot(grad_scores, q_h, 0, 0)
        scaled = (jnp.where(lanes, grad_out, 0.0) * inverse).astype(BF)
        dv += dot(weights.astype(BF), scaled, 0, 0)
    dq = (dq * HD**-0.5).astype(BF)
    dk = (dk * HD**-0.5).astype(BF)
    dv = dv.astype(BF)
    grads = jnp.concatenate([dq, dk, dv], axis=1)
    grad_ref[...] = grads
    sum_ref[0:1, :] = jnp.sum(dq.astype(F32), axis=0, keepdims=True)
    sum_ref[1:2, :] = jnp.sum(dv.astype(F32), axis=0, keepdims=True)
    part = dot(grads, w_ref[:, : 3 * 128], 1, 1)
    out_mine[...] = part[:256].astype(BF)
    out_other[...] = part[256:].astype(BF)


def gelu_parts(u):
    cubic = 0.044715 * u * u
    t = jnp.tanh(0.7978845608028654 * u * (1.0 + cubic))
    return t, cubic


def feed_body(*refs):
    rows = whole(refs[:8])
    w_ref, side_ref, out_mine, out_other, u_ref, z_ref = refs[8:]
    u = dot(rows, w_ref[:, :512]) + column_bias(side_ref, 8, 16)
    u_ref[...] = u
    t, _ = gelu_parts(u)
    z = (0.5 * u * (1.0 + t)).astype(BF)
    z_ref[...] = z
    part = dot(z, w_ref[:, 512:], 1, 1)
    out_mine[...] = part[:256].astype(BF)
    out_other[...] = part[256:].astype(BF)


def feed_back(grad_z, u):
    t, cubic = gelu_parts(u)
    slope = 0.5 * (1.0 + t) + 0.5 * u * (1.0 - t * t) * 0.7978845608028654 * (1.0 + 3.0 * cubic)
    return (grad_z * slope).astype(BF)


def feed_back_body(*refs):
    rows = whole(refs[:8])
    w_ref, u_ref, out_mine, out_other, du_ref, sum_ref = refs[8:]
    du = feed_back(dot(rows, w_ref[:, 512:]), u_ref[...])
    du_ref[...] = du
    sum_ref[...] = jnp.sum(du.astype(F32), axis=0, keepdims=True)
    part = dot(du, w_ref[:, :512], 1, 1)
    out_mine[...] = part[:256].astype(BF)
    out_other[...] = part[256:].astype(BF)


def feed_turn_body(*refs):
    rows, grad_rows = whole(refs[:8]), whole(refs[8:16], 64)
    w_ref, side_ref, out_mine, out_other, z_ref, du_ref, sum_ref = refs[16:]
    u = dot(rows, w_ref[:, :512]) + column_bias(side_ref, 8, 16)
    t, _ = gelu_parts(u)
    z = (0.5 * u * (1.0 + t)).astype(BF)
    z_ref[...] = z
    du = feed_back(dot(grad_rows, w_ref[:, 512:]), u)
    du_ref[...] = du
    sum_ref[...] = jnp.sum(du.astype(F32), axis=0, keepdims=True)
    for first, part in ((0, dot(z, w_ref[:, 512:], 1, 1)), (64, dot(du, w_ref[:, :512], 1, 1))):
        for j in range(4):
            rows = slice(128 * j + first, 128 * j + first + 64)
            out_mine[rows, :] = part[64 * j : 64 * j + 64].astype(BF)
            out_other[rows, :] = part[256 + 64 * j : 320 + 64 * j].astype(BF)


def mid_back(g, hidden, grad, par, dh_ref, low_ref, sums_ref):
    unit, rstd = norm_stats(hidden)
    dh = g + norm_back(grad, unit, rstd, par[1:2])
    low = dh.astype(BF)
    dh_ref[...] = dh
    low_ref[...] = low
    sums_ref[0:1, :] = jnp.sum(grad * unit, axis=0, keepdims=True)
    sums_ref[1:2, :] = jnp.sum(grad, axis=0, keepdims=True)
    sums_ref[2:3, :] = jnp.sum(low.astype(F32), axis=0, keepdims=True)
    sums_ref[3:4, :] = jnp.sum(g, axis=0, keepdims=True)


def mid_back_body(g_ref, hidden_ref, b0, b1, b2, b3, par_ref, dh_ref, low_ref, sums_ref):
    grad = total_of((b0, b1, b2, b3))
    mid_back(
        g_ref[...].astype(F32), hidden_ref[...], grad, par_ref[...].astype(F32), dh_ref, low_ref, sums_ref
    )


def turn_body(g_ref, hidden_ref, b0, b1, b2, b3, par_ref, act_ref, dh_ref, low_ref, sums_ref):
    total = total_of((b0, b1, b2, b3))
    par = par_ref[...].astype(F32)
    hidden = hidden_ref[...]
    act_ref[...] = (hidden + total[:64] + par[5:6]).astype(BF)
    mid_back(g_ref[...].astype(F32), hidden, total[64:], par, dh_ref, low_ref, sums_ref)


def end_back_body(dh_ref, x_ref, b0, b1, b2, b3, par_ref, out_ref, sums_ref):
    par = par_ref[...].astype(F32)
    grad = total_of((b0, b1, b2, b3))
    unit, rstd = norm_stats(x_ref[...].astype(F32))
    out_ref[...] = (dh_ref[...] + norm_back(grad, unit, rstd, par[0:1])).astype(BF)
    sums_ref[0:1, :] = jnp.sum(grad * unit, axis=0, keepdims=True)
    sums_ref[1:2, :] = jnp.sum(grad, axis=0, keepdims=True)


def feed_grads_body(*refs):
    g, b = whole(refs[:8]), whole(refs[8:16])
    du_ref, z_ref, out_ref = refs[16:]
    out_ref[:, :512] = dot(b, du_ref[...], 0, 0).astype(BF)
    out_ref[:, 512:] = dot(g, z_ref[...], 0, 0).astype(BF)


def other_places(y):
    flipped = y + 1 - 2 * lax.rem(y, 2)
    return flipped, 3 - y, 3 - flipped


def halving_messages(at_ref, full, keep, send):
    y = at_ref[3]
    flipped, mirrored, across = other_places(y)
    for half in range(2):
        rows = slice(128 * half, 128 * half + 128)
        for out, i, place in ((keep, 0, y), (keep, 1, mirrored), (send, 0, flipped), (send, 1, across)):
            out[i, rows, :] = full[pl.ds(pl.multiple_of((half * 4 + place) * 128, 128), 128), :]


def feed_grads(first, at_ref, refs):
    g, b = whole(refs[:8], first), whole(refs[8:16])
    du_ref, z_ref, *outs, full = refs[16:]
    full[:, :512] = dot(b, du_ref[...], 0, 0).astype(BF)
    full[:, 512:] = dot(g, z_ref[...], 0, 0).astype(BF)
    halving_messages(at_ref, full, *outs)


def attend_grads(refs, full):
    a, h = whole(refs[:8]), whole(refs[8:16])
    dqkv_ref, low_ref = refs[16:18]
    full[:, :384] = dot(a, dqkv_ref[...], 0, 0).astype(BF)
    full[:, 384:] = dot(h, low_ref[...], 0, 0).astype(BF)
    return a


def attend_grads_body(at_ref, *refs):
    attend_grads(refs, refs[-1])
    halving_messages(at_ref, refs[-1], *refs[18:20])


def halve_body(keep, came, mine, later):
    mine[...] = keep[0].astype(F32) + came[0].astype(F32)
    later[...] = (keep[1].astype(F32) + came[1].astype(F32)).astype(BF)


def halve_end_body(mine, came, out):
    out[...] = (mine[...] + came[...].astype(F32)).astype(BF)


def pack_body(at_ref, qkv_hbm, out_hbm, up_hbm, down_hbm, qv_hbm, upb_hbm, *refs):
    outs, held, sems = refs[:4], refs[4:10], refs[10]
    copies = [
        pltpu.make_async_copy(source, to, sems.at[i])
        for i, (source, to) in enumerate(
            zip((qkv_hbm, out_hbm, up_hbm, down_hbm, qv_hbm, upb_hbm), held)
        )
    ]
    for copy in copies:
        copy.start()
    for copy in copies:
        copy.wait()
    qkv_ref, out_ref, up_ref, down_ref, qv_ref, upb_ref = held
    qv = qv_ref[...].astype(F32)
    upb = upb_ref[...].astype(F32)

    def pick(row, first, count, start):
        n = row.shape[1]
        entry = lax.broadcasted_iota(jnp.int32, (n, 128), 0)
        lane = lax.broadcasted_iota(jnp.int32, (n, 128), 1)
        chosen = (entry == start + lane - first) & (lane >= first) & (lane < first + count)
        return dot(jnp.broadcast_to(row, (16, n)), chosen.astype(F32))

    for j in range(4):
        to = lax.rem(at_ref[0] + j, 4)
        narrow = pl.ds(pl.multiple_of(to * 128, 128), 128)
        broad = pl.ds(pl.multiple_of(to * 512, 512), 512)
        att = outs[j]
        for i in range(3):
            att[:32, 128 * i : 128 * i + 128] = qkv_ref[i, :, narrow]
        att[:32, 384:] = out_ref[:, narrow]
        side = pick(qv[0:1], 0, 4, 4 * to) + pick(qv[1:2], 4, 4, 4 * to) + pick(upb, 8, 16, 16 * to)
        att[32:48, :128] = side.astype(BF)
        att[32:48, 128:] = jnp.zeros((16, 384), BF)
        att[48:80, :] = up_ref[:, broad]
        att[80:, :] = down_ref[:, broad]


def collect_body(at_ref, *refs):
    att_ref, feed_ref = refs[4:]
    row = lax.broadcasted_iota(jnp.int32, (16, 512), 0)
    side = jnp.zeros((16, 512), F32)
    for j in range(4):
        place = lax.rem(at_ref[0] + 4 - j, 4)
        rows = pl.ds(pl.multiple_of(place * 32, 32), 32)
        att_ref[rows, :] = refs[j][:32, :]
        feed_ref[rows, :512] = refs[j][48:80, :]
        feed_ref[rows, 512:] = refs[j][80:, :]
        side = jnp.where(row == place, refs[j][32:48, :].astype(F32), side)
    att_ref[128:, :] = side.astype(BF)


def select_body(layer, at_ref, own, right, left, across, out):
    section, xh = at_ref[1], at_ref[2]
    out[xh] = jnp.where(section == layer, own[...], (right if layer else left)[...])
    out[1 - xh] = jnp.where(section == layer, across[...], (left if layer else right)[...])


def place_y_body(at_ref, *refs):
    for j in range(4):
        place = lax.rem(at_ref[3] + j, 4)
        for half in range(2):
            rows = pl.ds(pl.multiple_of((half * 4 + place) * 128, 128), 128)
            refs[4][rows, :] = refs[j][half, :128, :]
            if len(refs) > 5:
                rows = pl.ds(pl.multiple_of((half * 4 + place) * 16, 16), 16)
                refs[5][rows, :] = refs[j][half, 128:, :128]


def last_grads_body(at_ref, *refs):
    mine, other, par_ref, two0, one1, two1, qv0, u0, qv1, u1 = refs[18:28]
    outs, (sums, full) = refs[28:32], refs[32:]
    a = attend_grads(refs, full)
    par = par_ref[...].astype(F32)
    part = jnp.concatenate([mine[...], other[...]]).astype(F32)
    unit = (a.astype(F32) - par[2:3]) / par[0:1]
    sums[...] = jnp.zeros((16, D), F32)
    sums[0:1, :] = jnp.sum(part * unit, axis=0, keepdims=True)
    sums[1:2, :] = two0[0:1, :]
    sums[2:3, :] = jnp.sum(part, axis=0, keepdims=True)
    sums[3:6, :] = two0[1:4, :]
    sums[6:7, :] = one1[0:1, :]
    sums[7:8, :] = two1[0:1, :]
    sums[8:9, :] = one1[1:2, :]
    sums[9:12, :] = two1[1:4, :]
    for row, qv, u in ((12, qv0, u0), (13, qv1, u1)):
        sums[row : row + 1, :128] = qv[0:1, :]
        sums[row : row + 1, 128:256] = qv[1:2, :]
        sums[row : row + 1, 256:768] = u[...]
    low = sums[...].astype(BF)
    for j, out in enumerate(outs):
        place = lax.rem(at_ref[3] + j, 4)
        for half in range(2):
            rows = pl.ds(pl.multiple_of((half * 4 + place) * 128, 128), 128)
            out[128 * half : 128 * half + 128, :] = full[rows, :]
        out[256:272, :] = low[:, :512]
        out[272:288, :] = low[:, 512:]


def sum_of(refs):
    total = refs[0][...].astype(F32)
    for ref in refs[1:]:
        total = total + ref[...].astype(F32)
    return total


def target_x(at_ref, j):
    x = lax.rem(at_ref[2] * 2 + at_ref[1] + j, 4)
    return lax.rem(x, 2), x // 2


def feed_blocks_body(at_ref, first, second, *outs):
    for j, out in enumerate(outs):
        layer, half = target_x(at_ref, j)
        rows = pl.ds(pl.multiple_of(half * 128, 128), 128)
        out[...] = jnp.where(layer == 0, first[rows, :], second[rows, :])


def attend_blocks_body(at_ref, m0, m1, m2, m3, second, *outs):
    total = sum_of((m0, m1, m2, m3))
    low = total.astype(BF)
    for j, out in enumerate(outs):
        layer, half = target_x(at_ref, j)
        own = jnp.where(half == 0, low[:128], low[128:256])
        rows = pl.ds(pl.multiple_of(half * 128, 128), 128)
        out[:128, :] = jnp.where(layer == 0, own, second[rows, :])
        out[128:, :] = low[256:]


def z_blocks_body(at_ref, a0, a1, a2, a3, f0, f1, f2, f3, o0, o1, o2, o3, rows_ref):
    att = sum_of((a0, a1, a2, a3)).astype(BF)
    rows_ref[:, :512] = att[:128]
    rows_ref[:, 512:] = sum_of((f0, f1, f2, f3)).astype(BF)
    for j, out in enumerate((o0, o1, o2, o3)):
        to = lax.rem(at_ref[0] + j, 4)
        out[:32, :] = rows_ref[pl.ds(pl.multiple_of(to * 32, 32), 32), :]
        out[32:, :512] = att[128:144]
        out[32:, 512:1024] = att[144:160]
        out[32:, 1024:] = jnp.zeros((16, 512), BF)


def finish_body(at_ref, m0, m1, m2, m3, qkv_ref, out_ref, up_ref, down_ref, vector_ref, side_ref):
    row = lax.broadcasted_iota(jnp.int32, (8, 768), 0)
    total = jnp.zeros((16, D), F32)
    side = jnp.zeros((8, 768), F32)
    section = at_ref[1]
    for j, ref in enumerate((m0, m1, m2, m3)):
        place = lax.rem(at_ref[0] + 4 - j, 4)
        narrow = pl.ds(pl.multiple_of(place * 128, 128), 128)
        broad = pl.ds(pl.multiple_of(place * 512, 512), 512)
        for i in range(3):
            qkv_ref[i, :, narrow] = ref[:32, 128 * i : 128 * i + 128].astype(F32)
        out_ref[:, narrow] = ref[:32, 384:512].astype(F32)
        up_ref[:, broad] = ref[:32, 512:1024].astype(F32)
        down_ref[:, broad] = ref[:32, 1024:].astype(F32)
        sums = ref[32:, :1024].astype(F32)
        total = total + sums
        own = jnp.where(section == 0, sums[12:13, :768], sums[13:14, :768])
        side = jnp.where(row == place, own, side)
    vector_ref[...] = jnp.where(section == 0, total[:6], total[6:12])
    index = (at_ref[2] * 4 + at_ref[3]) * 4 + at_ref[0]
    entry = lax.broadcasted_iota(jnp.int32, (8, 768), 1)
    kept = jnp.where(entry % 32 == index, side, 0.0)
    entry = lax.broadcasted_iota(jnp.int32, (768, 128), 0)
    lane = lax.broadcasted_iota(jnp.int32, (768, 128), 1)
    side_ref[...] = dot(kept, (entry // 32 == lane).astype(F32))


def shards(inputs, cotangent, segments, qkv_weight, out_weight, up_weight, down_weight, norm_gains, biases, qv_bias, up_bias):
    section, xh, y, z = (lax.axis_index(name) for name in ("section", "xh", "y", "z"))
    core = lax.axis_index("tensor")
    at = jnp.stack([z, section, xh, y]).astype(jnp.int32)
    x0 = lax.dynamic_index_in_dim(inputs, section, 0, keepdims=False)
    g1 = lax.dynamic_index_in_dim(cotangent, section, 0, keepdims=False)
    own_par = jnp.concatenate([norm_gains[0], biases[0]])
    other_par = swap(own_par, "section")

    sources = (
        qkv_weight[0], out_weight[0].T, up_weight[0], down_weight[0].T, qv_bias[0, :, :, 0], up_bias[0].T
    )
    packed = call(
        pack_body,
        [((112, ATT), BF)] * 4,
        at, *sources,
        scalars=1,
        outside=True,
        vmem=56,
        scratch=[pltpu.VMEM(a.shape, BF) for a in sources] + [pltpu.SemaphoreType.DMA((6,))],
    )
    came = [packed[0]] + [shift(packed[j], "z", -j) for j in (1, 2, 3)]
    att_rows, feed_rows = call(
        collect_body, [((144, ATT), BF), ((128, MLP), BF)], at, *came, scalars=1
    )

    def along_x(part):
        return [part] + [x_shift(part, j) for j in (1, 3, 2)]

    def along_y(layer, pieces, after=()):
        body = lambda *refs: select_body(layer, *refs)
        (rows,) = call(
            body, [((2, *pieces[0].shape), BF)], at, *pieces, scalars=1, after=after
        )
        return [rows] + [shift(rows, "y", j) for j in (1, 2, 3)]

    att_outs = [((D, ATT), BF), ((128, 128), BF)]
    feed_outs = [((D, MLP), BF)]
    att_x = along_x(att_rows)
    att_y = along_y(0, att_x)
    feed_x = along_x(feed_rows)

    row = lax.dynamic_index_in_dim(segments, section, 0, keepdims=False)
    run = lax.dynamic_slice_in_dim(row, (xh * 4 + y) * RUN, RUN)
    marks = jnp.stack([jnp.arange(RUN, dtype=jnp.int32), run]).reshape(2, 4, 2, 64)
    marks = lax.dynamic_slice_in_dim(jnp.concatenate([marks, marks], axis=1), z, 4, 1)
    marks = jnp.where(core == 0, marks, marks[:, :, ::-1])
    marks = jnp.transpose(marks, (0, 2, 1, 3)).reshape(2, RUN)
    allowed = (marks[0][None, :] <= marks[0][:, None]) & (marks[1][None, :] == marks[1][:, None])
    mask = jnp.where(allowed, 0.0, MASKED).astype(F32)

    pars = [
        jnp.where(section == 0, own_par, other_par),
        jnp.where(section == 0, other_par, own_par),
    ]

    half = [((256, D), BF)] * 2
    saved = []
    acts = [None, None]
    weights = []
    rows = x0
    normed = call(first_norm_body, [((128, D), BF)], x0, g1, pars[0])[0]
    for layer in (0, 1):
        par = pars[layer]
        a_rows = gather_rows(normed)
        if layer == 0:
            g_rows = a_rows
            att, side = call(
                place_y_body, att_outs, at, *att_y, scalars=1, after=[*a_rows, mask]
            )
        else:
            att, side = call(
                place_y_body, att_outs, at, *att_y, scalars=1, after=a_rows[:4]
            )
        feed_y = along_y(layer, feed_x, after=(rows,) if layer else (att,))
        *parts, qkv, attended, att_low = call(
            attend_body,
            half + [((3, RUN, 128), BF), ((RUN, 128), F32), ((RUN, 128), BF)],
            *a_rows, att, side, mask, after=(feed_y[0],),
        )
        blocks, added = scatter_rows(*parts)
        hidden, second = call(
            mid_body, [((64, D), F32), ((64, D), BF)], rows, *blocks, par
        )
        b_rows = gather_rows(second)
        (feed,) = call(place_y_body, feed_outs, at, *feed_y, scalars=1, after=b_rows[:4])
        weights.append((att, feed))
        if layer == 0:
            att_y = along_y(1, att_x, after=(feed,))
            *parts, u, gelu_low = call(
                feed_body,
                half + [((RUN, 512), F32), ((RUN, 512), BF)],
                *b_rows, feed, side, after=(att_y[0],),
            )
            blocks, added = scatter_rows(*parts)
            saved.append((rows, a_rows, qkv, attended, att_low, hidden, b_rows, u, gelu_low))
            rows, normed = call(
                end_body, [((64, D), BF)] * 2, hidden, *blocks, par, pars[1]
            )
            acts[0] = rows

    inputs_back = [None, None]
    sums_two = [None, None]
    sums_one = [None, None]
    u_sum = [None, None]
    qv_sum = [None, None]
    feed_sums = [None, None]
    grad_rows = g1

    def halve(messages, after):
        keep, send = messages
        shape = keep.shape[1:]
        mine, later = call(halve_body, [(shape, F32), (shape, BF)], keep, flip(send), after=after)
        return mine, mirror(later)

    def halve_end(pieces, after):
        return call(halve_end_body, [(pieces[0].shape, BF)], *pieces, after=after)[0]

    def message_shapes(n):
        return [((2, 256, n), BF)] * 2

    for layer in (1, 0):
        att, feed = weights[layer]
        par = pars[layer]
        if layer:
            *parts, gelu_low, du, u_sum[1] = call(
                feed_turn_body,
                [((512, D), BF)] * 2 + [((RUN, 512), BF)] * 2 + [((1, 512), F32)],
                *b_rows, *g_rows, feed, side,
            )
            blocks, added = scatter_rows(*parts)
            order = (added,)
        else:
            rows, a_rows, qkv, attended, att_low, hidden, b_rows, u, gelu_low = saved[0]
            g_rows = gather_rows(grad_rows)
            att_step = halve(att_messages, after=())
            *parts, du, u_sum[0] = call(
                feed_back_body, half + [((RUN, 512), BF), ((1, 512), F32)], *g_rows, feed, u,
                after=(feed_sums[1], att_step[0]),
            )
            blocks, added = scatter_rows(*parts)
            grad_att = halve_end(att_step, after=(added,))
            order = (added,)
        body = lambda at_ref, *refs, first=64 * layer: feed_grads(first, at_ref, refs)
        messages = call(
            body, message_shapes(MLP), at, *g_rows, *b_rows, du, gelu_low,
            scalars=1, flops=4 * RUN * D * 512, after=order, scratch=[pltpu.VMEM((D, MLP), BF)],
        )
        if layer:
            acts[1], dh, dh_low, sums_two[1] = call(
                turn_body,
                [((64, D), BF), ((64, D), F32), ((64, D), BF), ((4, D), F32)],
                grad_rows, hidden, *blocks, par, after=(messages[0],),
            )
        else:
            dh, dh_low, sums_two[0] = call(
                mid_back_body,
                [((64, D), F32), ((64, D), BF), ((4, D), F32)],
                grad_rows, hidden, *blocks, par, after=(messages[0],),
            )
        h_rows = gather_rows(dh_low)
        *parts, dqkv, qv_sum[layer] = call(
            attend_back_body,
            half + [((RUN, 384), BF), ((2, 128), F32)],
            *h_rows, att, mask, qkv, attended, after=() if layer else (grad_att,),
        )
        feed_step = halve(messages, after=(dqkv,))
        if layer == 0:
            last = call(
                last_grads_body,
                [((288, ATT), BF)] * 4,
                at, *a_rows, *h_rows, dqkv, att_low, *parts, pars[0],
                sums_two[0], sums_one[1], sums_two[1], qv_sum[0], u_sum[0], qv_sum[1], u_sum[1],
                scalars=1, after=(feed_step[0],), scratch=[pltpu.VMEM((16, D), F32), pltpu.VMEM((D, ATT), BF)],
            )
        blocks, added = scatter_rows(*parts, after=(feed_step[0],) if layer else ())
        feed_sums[layer] = halve_end(feed_step, after=(added,) if layer else (last[0],))
        if layer:
            att_messages = call(
                attend_grads_body, message_shapes(ATT), at, *a_rows, *h_rows, dqkv, att_low,
                scalars=1, flops=2 * RUN * D * 512, after=(added,),
                scratch=[pltpu.VMEM((D, ATT), BF)],
            )
        grad_rows, sums_one[layer] = call(
            end_back_body, [((64, D), BF), ((2, D), F32)], dh, rows, *blocks, par,
            after=(att_messages[0],) if layer else (),
        )
        inputs_back[layer] = grad_rows

    messages = last[:4]
    feed_out = call(
        feed_blocks_body, [((128, MLP), BF)] * 4, at, *feed_sums, scalars=1, after=(messages[0],)
    )
    feed_in = [feed_out[0]] + [x_shift(feed_out[j], -j) for j in (1, 2, 3)]
    att_in = [messages[0]] + [shift(messages[j], "y", -j) for j in (1, 2, 3)]
    att_out = call(
        attend_blocks_body, [((160, ATT), BF)] * 4, at, *att_in, grad_att, scalars=1, after=(feed_in[1], feed_in[2])
    )
    att_in = [att_out[0]] + [x_shift(att_out[j], -j) for j in (1, 2, 3)]
    *out, _ = call(
        z_blocks_body,
        [((48, 1536), BF)] * 4 + [((128, 1536), BF)],
        at, *att_in, *feed_in, scalars=1, after=(grad_rows,),
    )
    came = [out[0]] + [shift(out[j], "z", -j) for j in (1, 2, 3)]
    grad_qkv, grad_out, grad_up, grad_down, vector, side = call(
        finish_body,
        [((3, 32, 512), F32), ((32, 512), F32), ((32, 2048), F32), ((32, 2048), F32), ((6, D), F32), ((8, 128), F32)],
        at, *came, scalars=1,
    )
    vector = vector + swap(vector, "tensor")
    grad_qv = jnp.transpose(side[:4, :8].reshape(4, 2, 4), (1, 0, 2)).reshape(1, 2, 16, 1)
    grad_upb = side[:4, 8:24].reshape(1, 64, 1)

    def own_layer(per_layer):
        kept = jnp.where(section == 0, per_layer[0], per_layer[1])
        sent = swap(jnp.where(section == 0, per_layer[1], per_layer[0]), "section")
        return jnp.stack(
            [jnp.where(section == 0, kept, sent), jnp.where(section == 0, sent, kept)]
        )[None]

    return (
        own_layer(acts),
        own_layer(inputs_back),
        grad_qkv[None],
        grad_out.T[None],
        grad_up[None],
        grad_down.T[None],
        vector[None, 0:2],
        vector[None, 2:6],
        grad_qv,
        grad_upb,
    )


def solution(mesh):
    fine = Mesh(mesh.devices.reshape(2, 2, 4, 4, 2), ("section", "xh", "y", "z", "tensor"))
    dp = ("xh", "y", "z")
    return jax.shard_map(
        shards,
        mesh=fine,
        in_specs=(
            P(None, (*dp, "tensor"), None),
            P(None, (*dp, "tensor"), None),
            P(),
            P("section", None, dp, "tensor"),
            P("section", "tensor", dp),
            P("section", dp, "tensor"),
            P("section", "tensor", dp),
            P("section", None, None),
            P("section", None, None),
            P("section", None, "tensor", dp),
            P("section", "tensor", dp),
        ),
        out_specs=(
            P("section", None, (*dp, "tensor"), None),
            P("section", None, (*dp, "tensor"), None),
            P("section", None, dp, "tensor"),
            P("section", "tensor", dp),
            P("section", dp, "tensor"),
            P("section", "tensor", dp),
            P("section", None, None),
            P("section", None, None),
            P("section", None, "tensor", dp),
            P("section", "tensor", dp),
        ),
        check_vma=False,
    )
```

```python
import jax
import jax.numpy as jnp
from jax import lax
from jax.experimental import pallas as pl
from jax.experimental.pallas import tpu as pltpu
from jax.sharding import Mesh, PartitionSpec as P

D = 1024
HD = 64
VEC = 32
RUN = 512
EPS = 1e-05
MASKED = -1e30
BF = jnp.bfloat16
F32 = jnp.float32
ATT = 512
MLP = 1024
MIB = 1024 * 1024


def call(body, outs, *args, flops=0, scalars=0, after=(), vmem=16, scratch=(), outside=False):
    space = pltpu.HBM if outside else pltpu.VMEM
    specs = [pl.BlockSpec(memory_space=pltpu.SMEM)] * scalars
    specs += [pl.BlockSpec(memory_space=space)] * (len(args) - scalars)
    specs += [pl.BlockSpec(memory_space=pl.ANY)] * len(after)
    count = len(args)

    def kernel(*refs):
        body(*refs[:count], *refs[count + len(after) :])

    return pl.pallas_call(
        kernel,
        out_shape=[jax.ShapeDtypeStruct(shape, dtype) for shape, dtype in outs],
        in_specs=specs,
        out_specs=[pl.BlockSpec(memory_space=pltpu.VMEM)] * len(outs),
        scratch_shapes=list(scratch),
        compiler_params=pltpu.CompilerParams(vmem_limit_bytes=vmem * MIB),
        cost_estimate=pl.CostEstimate(
            flops=flops, bytes_accessed=MIB // 8, transcendentals=0
        ),
    )(*args, *after)


def dot(a, b, ca=1, cb=0):
    return lax.dot_general(a, b, (((ca,), (cb,)), ((), ())), preferred_element_type=F32)


def shift(array, axis, by, size=4):
    return lax.ppermute(array, axis, [((i + by) % size, i) for i in range(size)])


def x_shift(array, by):
    def rank(x):
        return (x % 2) * 2 + x // 2

    pairs = [(rank((x + by) % 4), rank(x)) for x in range(4)]
    return lax.ppermute(array, ("section", "xh"), pairs)


def flip(array):
    return lax.ppermute(array, "y", [(i, i ^ 1) for i in range(4)])


def mirror(array):
    return lax.ppermute(array, "y", [(i, 3 - i) for i in range(4)])


def swap(array, axis):
    return lax.ppermute(array, axis, [(0, 1), (1, 0)])


def gather_rows(rows):
    across, *sides = [shift(rows, "z", j) for j in (2, 1, 3)]
    mine = [rows, sides[0], across, sides[1]]
    return mine + [swap(piece, "tensor") for piece in mine]


def whole(refs, first=0):
    return jnp.concatenate([ref[first : first + 64, :] for ref in refs])


def add_body(mine_ref, other_ref, *outs):
    n = outs[0].shape[0]
    for j, out in enumerate(outs):
        rows = pl.ds(n * j, n)
        total = mine_ref[rows, :].astype(F32) + other_ref[rows, :].astype(F32)
        out[...] = total.astype(out.dtype)


def scatter_rows(mine, other, after=()):
    arrived = swap(other, "tensor")
    n = mine.shape[0] // 4
    blocks = call(
        add_body, [((n, D), F32)] + [((n, D), BF)] * 3, mine, arrived, after=after
    )
    return [blocks[0]] + [shift(blocks[j], "z", -j) for j in (2, 1, 3)], blocks[1]


def norm_stats(values):
    centred = values - jnp.mean(values, axis=-1, keepdims=True)
    rstd = lax.rsqrt(jnp.mean(centred * centred, axis=-1, keepdims=True) + EPS)
    return centred * rstd, rstd


def norm_back(grad, unit, rstd, gain):
    scaled = grad * gain
    return rstd * (
        scaled
        - jnp.mean(scaled, axis=-1, keepdims=True)
        - unit * jnp.mean(scaled * unit, axis=-1, keepdims=True)
    )


def total_of(refs):
    total = refs[0][...]
    for ref in refs[1:]:
        total = total + ref[...].astype(F32)
    return total


def first_norm_body(x_ref, g_ref, par_ref, out_ref):
    unit, _ = norm_stats(x_ref[...].astype(F32))
    par = par_ref[...].astype(F32)
    out_ref[:64, :] = (unit * par[0:1] + par[2:3]).astype(BF)
    out_ref[64:, :] = g_ref[...]


def mid_body(x_ref, b0, b1, b2, b3, par_ref, hidden_ref, out_ref):
    par = par_ref[...].astype(F32)
    hidden = x_ref[...].astype(F32) + total_of((b0, b1, b2, b3)) + par[4:5]
    hidden_ref[...] = hidden
    unit, _ = norm_stats(hidden)
    out_ref[...] = (unit * par[1:2] + par[3:4]).astype(BF)


def end_body(hidden_ref, b0, b1, b2, b3, par_ref, next_ref, act_ref, out_ref):
    par = par_ref[...].astype(F32)
    act = (hidden_ref[...] + total_of((b0, b1, b2, b3)) + par[5:6]).astype(BF)
    act_ref[...] = act
    unit, _ = norm_stats(act.astype(F32))
    later = next_ref[...].astype(F32)
    out_ref[...] = (unit * later[0:1] + later[2:3]).astype(BF)


def head_lanes(h):
    lane = lax.broadcasted_iota(jnp.int32, (1, 2 * HD), 1)
    return (lane >= h * HD) & (lane < (h + 1) * HD)


def column_bias(side_ref, first, count):
    side = side_ref[...].reshape(8, 16, 128)[:, :4].reshape(32, 128)
    n = 32 * count
    lane = lax.broadcasted_iota(jnp.int32, (128, n), 0)
    entry = lax.broadcasted_iota(jnp.int32, (128, n), 1)
    spread = dot(side, (lane == first + entry // 32).astype(F32))
    device = lax.broadcasted_iota(jnp.int32, (32, n), 0)
    entry = lax.broadcasted_iota(jnp.int32, (32, n), 1)
    return jnp.sum(jnp.where(entry % 32 == device, spread, 0.0), axis=0, keepdims=True)


def attend_body(*refs):
    rows = whole(refs[:8])
    w_ref, side_ref, mask_ref, out_mine, out_other, qkv_ref, att_ref, low_ref = refs[8:]
    projected = dot(rows, w_ref[:, : 3 * 128])
    q = (projected[:, :128] + column_bias(side_ref, 0, 4)).astype(BF)
    k = projected[:, 128:256].astype(BF)
    v = (projected[:, 256:] + column_bias(side_ref, 4, 4)).astype(BF)
    qkv_ref[0] = q
    qkv_ref[1] = k
    qkv_ref[2] = v
    zero = jnp.zeros((), BF)
    attended = jnp.zeros((RUN, 128), F32)
    for h in range(2):
        lanes = head_lanes(h)
        scores = dot(jnp.where(lanes, q, zero), k, 1, 1) * HD**-0.5 + mask_ref[...]
        weights = jnp.exp(scores - jnp.max(scores, axis=-1, keepdims=True))
        total = jnp.sum(weights, axis=-1, keepdims=True)
        attended += dot(weights.astype(BF), jnp.where(lanes, v, zero)) / total
    att_ref[...] = attended
    low = attended.astype(BF)
    low_ref[...] = low
    part = dot(low, w_ref[:, 384:512], 1, 1)
    out_mine[...] = part[:256].astype(BF)
    out_other[...] = part[256:].astype(BF)


def attend_back_body(*refs):
    rows = whole(refs[:8])
    w_ref, mask_ref, qkv_ref, att_ref, out_mine, out_other, grad_ref, sum_ref = refs[8:]
    grad_low = dot(rows, w_ref[:, 384:512]).astype(BF)
    grad_out = grad_low.astype(F32)
    q, k, v = qkv_ref[0], qkv_ref[1], qkv_ref[2]
    zero = jnp.zeros((), BF)
    products = grad_out * att_ref[...]
    dq = jnp.zeros((RUN, 128), F32)
    dk = jnp.zeros((RUN, 128), F32)
    dv = jnp.zeros((RUN, 128), F32)
    for h in range(2):
        lanes = head_lanes(h)
        q_h = jnp.where(lanes, q, zero)
        scores = dot(q_h, k, 1, 1) * HD**-0.5 + mask_ref[...]
        weights = jnp.exp(scores - jnp.max(scores, axis=-1, keepdims=True))
        inverse = 1.0 / jnp.sum(weights, axis=-1, keepdims=True)
        delta = jnp.sum(jnp.where(lanes, products, 0.0), axis=-1, keepdims=True)
        grad_h = jnp.where(lanes, grad_low, zero)
        grad_probs = dot(grad_h, v, 1, 1)
        grad_scores = (weights * inverse * (grad_probs - delta)).astype(BF)
        dq += dot(grad_scores, jnp.where(lanes, k, zero))
        dk += dot(grad_scores, q_h, 0, 0)
        scaled = (jnp.where(lanes, grad_out, 0.0) * inverse).astype(BF)
        dv += dot(weights.astype(BF), scaled, 0, 0)
    dq = (dq * HD**-0.5).astype(BF)
    dk = (dk * HD**-0.5).astype(BF)
    dv = dv.astype(BF)
    grads = jnp.concatenate([dq, dk, dv], axis=1)
    grad_ref[...] = grads
    sum_ref[0:1, :] = jnp.sum(dq.astype(F32), axis=0, keepdims=True)
    sum_ref[1:2, :] = jnp.sum(dv.astype(F32), axis=0, keepdims=True)
    part = dot(grads, w_ref[:, : 3 * 128], 1, 1)
    out_mine[...] = part[:256].astype(BF)
    out_other[...] = part[256:].astype(BF)


def gelu_parts(u):
    cubic = 0.044715 * u * u
    t = jnp.tanh(0.7978845608028654 * u * (1.0 + cubic))
    return t, cubic


def feed_body(*refs):
    rows = whole(refs[:8])
    w_ref, side_ref, out_mine, out_other, u_ref, z_ref = refs[8:]
    u = dot(rows, w_ref[:, :512]) + column_bias(side_ref, 8, 16)
    u_ref[...] = u
    t, _ = gelu_parts(u)
    z = (0.5 * u * (1.0 + t)).astype(BF)
    z_ref[...] = z
    part = dot(z, w_ref[:, 512:], 1, 1)
    out_mine[...] = part[:256].astype(BF)
    out_other[...] = part[256:].astype(BF)


def feed_back(grad_z, u):
    t, cubic = gelu_parts(u)
    slope = 0.5 * (1.0 + t) + 0.5 * u * (1.0 - t * t) * 0.7978845608028654 * (1.0 + 3.0 * cubic)
    return (grad_z * slope).astype(BF)


def feed_back_body(*refs):
    rows = whole(refs[:8])
    w_ref, u_ref, out_mine, out_other, du_ref, sum_ref = refs[8:]
    du = feed_back(dot(rows, w_ref[:, 512:]), u_ref[...])
    du_ref[...] = du
    sum_ref[...] = jnp.sum(du.astype(F32), axis=0, keepdims=True)
    part = dot(du, w_ref[:, :512], 1, 1)
    out_mine[...] = part[:256].astype(BF)
    out_other[...] = part[256:].astype(BF)


def feed_turn_body(*refs):
    rows, grad_rows = whole(refs[:8]), whole(refs[8:16], 64)
    w_ref, side_ref, out_mine, out_other, z_ref, du_ref, sum_ref = refs[16:]
    u = dot(rows, w_ref[:, :512]) + column_bias(side_ref, 8, 16)
    t, _ = gelu_parts(u)
    z = (0.5 * u * (1.0 + t)).astype(BF)
    z_ref[...] = z
    du = feed_back(dot(grad_rows, w_ref[:, 512:]), u)
    du_ref[...] = du
    sum_ref[...] = jnp.sum(du.astype(F32), axis=0, keepdims=True)
    for first, part in ((0, dot(z, w_ref[:, 512:], 1, 1)), (64, dot(du, w_ref[:, :512], 1, 1))):
        for j in range(4):
            rows = slice(128 * j + first, 128 * j + first + 64)
            out_mine[rows, :] = part[64 * j : 64 * j + 64].astype(BF)
            out_other[rows, :] = part[256 + 64 * j : 320 + 64 * j].astype(BF)


def mid_back(g, hidden, grad, par, dh_ref, low_ref, sums_ref):
    unit, rstd = norm_stats(hidden)
    dh = g + norm_back(grad, unit, rstd, par[1:2])
    low = dh.astype(BF)
    dh_ref[...] = dh
    low_ref[...] = low
    sums_ref[0:1, :] = jnp.sum(grad * unit, axis=0, keepdims=True)
    sums_ref[1:2, :] = jnp.sum(grad, axis=0, keepdims=True)
    sums_ref[2:3, :] = jnp.sum(low.astype(F32), axis=0, keepdims=True)
    sums_ref[3:4, :] = jnp.sum(g, axis=0, keepdims=True)


def mid_back_body(g_ref, hidden_ref, b0, b1, b2, b3, par_ref, dh_ref, low_ref, sums_ref):
    grad = total_of((b0, b1, b2, b3))
    mid_back(
        g_ref[...].astype(F32), hidden_ref[...], grad, par_ref[...].astype(F32), dh_ref, low_ref, sums_ref
    )


def turn_body(g_ref, hidden_ref, b0, b1, b2, b3, par_ref, act_ref, dh_ref, low_ref, sums_ref):
    total = total_of((b0, b1, b2, b3))
    par = par_ref[...].astype(F32)
    hidden = hidden_ref[...]
    act_ref[...] = (hidden + total[:64] + par[5:6]).astype(BF)
    mid_back(g_ref[...].astype(F32), hidden, total[64:], par, dh_ref, low_ref, sums_ref)


def end_back_body(dh_ref, x_ref, b0, b1, b2, b3, par_ref, out_ref, sums_ref):
    par = par_ref[...].astype(F32)
    grad = total_of((b0, b1, b2, b3))
    unit, rstd = norm_stats(x_ref[...].astype(F32))
    out_ref[...] = (dh_ref[...] + norm_back(grad, unit, rstd, par[0:1])).astype(BF)
    sums_ref[0:1, :] = jnp.sum(grad * unit, axis=0, keepdims=True)
    sums_ref[1:2, :] = jnp.sum(grad, axis=0, keepdims=True)


def feed_grads_body(*refs):
    g, b = whole(refs[:8]), whole(refs[8:16])
    du_ref, z_ref, out_ref = refs[16:]
    out_ref[:, :512] = dot(b, du_ref[...], 0, 0).astype(BF)
    out_ref[:, 512:] = dot(g, z_ref[...], 0, 0).astype(BF)


def other_places(y):
    flipped = y + 1 - 2 * lax.rem(y, 2)
    return flipped, 3 - y, 3 - flipped


def halving_messages(at_ref, full, keep, send):
    y = at_ref[3]
    flipped, mirrored, across = other_places(y)
    for half in range(2):
        rows = slice(128 * half, 128 * half + 128)
        for out, i, place in ((keep, 0, y), (keep, 1, mirrored), (send, 0, flipped), (send, 1, across)):
            out[i, rows, :] = full[pl.ds(pl.multiple_of((half * 4 + place) * 128, 128), 128), :]


def feed_grads(first, at_ref, refs):
    g, b = whole(refs[:8], first), whole(refs[8:16])
    du_ref, z_ref, *outs, full = refs[16:]
    full[:, :512] = dot(b, du_ref[...], 0, 0).astype(BF)
    full[:, 512:] = dot(g, z_ref[...], 0, 0).astype(BF)
    halving_messages(at_ref, full, *outs)


def attend_grads(refs, full):
    a, h = whole(refs[:8]), whole(refs[8:16])
    dqkv_ref, low_ref = refs[16:18]
    full[:, :384] = dot(a, dqkv_ref[...], 0, 0).astype(BF)
    full[:, 384:] = dot(h, low_ref[...], 0, 0).astype(BF)
    return a


def attend_grads_body(at_ref, *refs):
    attend_grads(refs, refs[-1])
    halving_messages(at_ref, refs[-1], *refs[18:20])


def halve_body(keep, came, mine, later):
    mine[...] = keep[0].astype(F32) + came[0].astype(F32)
    later[...] = (keep[1].astype(F32) + came[1].astype(F32)).astype(BF)


def halve_end_body(mine, came, out):
    out[...] = (mine[...] + came[...].astype(F32)).astype(BF)


def pack_body(at_ref, qkv_hbm, out_hbm, up_hbm, down_hbm, qv_hbm, upb_hbm, *refs):
    outs, held, sems = refs[:4], refs[4:10], refs[10]
    copies = [
        pltpu.make_async_copy(source, to, sems.at[i])
        for i, (source, to) in enumerate(
            zip((qkv_hbm, out_hbm, up_hbm, down_hbm, qv_hbm, upb_hbm), held)
        )
    ]
    for copy in copies:
        copy.start()
    for copy in copies:
        copy.wait()
    qkv_ref, out_ref, up_ref, down_ref, qv_ref, upb_ref = held
    qv = qv_ref[...].astype(F32)
    upb = upb_ref[...].astype(F32)

    def pick(row, first, count, start):
        n = row.shape[1]
        entry = lax.broadcasted_iota(jnp.int32, (n, 128), 0)
        lane = lax.broadcasted_iota(jnp.int32, (n, 128), 1)
        chosen = (entry == start + lane - first) & (lane >= first) & (lane < first + count)
        return dot(jnp.broadcast_to(row, (16, n)), chosen.astype(F32))

    for j in range(4):
        to = lax.rem(at_ref[0] + j, 4)
        narrow = pl.ds(pl.multiple_of(to * 128, 128), 128)
        broad = pl.ds(pl.multiple_of(to * 512, 512), 512)
        att = outs[j]
        for i in range(3):
            att[:32, 128 * i : 128 * i + 128] = qkv_ref[i, :, narrow]
        att[:32, 384:] = out_ref[:, narrow]
        side = pick(qv[0:1], 0, 4, 4 * to) + pick(qv[1:2], 4, 4, 4 * to) + pick(upb, 8, 16, 16 * to)
        att[32:48, :128] = side.astype(BF)
        att[32:48, 128:] = jnp.zeros((16, 384), BF)
        att[48:80, :] = up_ref[:, broad]
        att[80:, :] = down_ref[:, broad]


def collect_body(at_ref, *refs):
    att_ref, feed_ref = refs[4:]
    row = lax.broadcasted_iota(jnp.int32, (16, 512), 0)
    side = jnp.zeros((16, 512), F32)
    for j in range(4):
        place = lax.rem(at_ref[0] + 4 - j, 4)
        rows = pl.ds(pl.multiple_of(place * 32, 32), 32)
        att_ref[rows, :] = refs[j][:32, :]
        feed_ref[rows, :512] = refs[j][48:80, :]
        feed_ref[rows, 512:] = refs[j][80:, :]
        side = jnp.where(row == place, refs[j][32:48, :].astype(F32), side)
    att_ref[128:, :] = side.astype(BF)


def select_body(layer, at_ref, own, right, left, across, out):
    section, xh = at_ref[1], at_ref[2]
    out[xh] = jnp.where(section == layer, own[...], (right if layer else left)[...])
    out[1 - xh] = jnp.where(section == layer, across[...], (left if layer else right)[...])


def place_y_body(at_ref, *refs):
    for j in range(4):
        place = lax.rem(at_ref[3] + j, 4)
        for half in range(2):
            rows = pl.ds(pl.multiple_of((half * 4 + place) * 128, 128), 128)
            refs[4][rows, :] = refs[j][half, :128, :]
            if len(refs) > 5:
                rows = pl.ds(pl.multiple_of((half * 4 + place) * 16, 16), 16)
                refs[5][rows, :] = refs[j][half, 128:, :128]


def last_grads_body(at_ref, *refs):
    mine, other, par_ref, two0, one1, two1, qv0, u0, qv1, u1 = refs[18:28]
    outs, (sums, full) = refs[28:32], refs[32:]
    a = attend_grads(refs, full)
    par = par_ref[...].astype(F32)
    part = jnp.concatenate([mine[...], other[...]]).astype(F32)
    unit = (a.astype(F32) - par[2:3]) / par[0:1]
    sums[...] = jnp.zeros((16, D), F32)
    sums[0:1, :] = jnp.sum(part * unit, axis=0, keepdims=True)
    sums[1:2, :] = two0[0:1, :]
    sums[2:3, :] = jnp.sum(part, axis=0, keepdims=True)
    sums[3:6, :] = two0[1:4, :]
    sums[6:7, :] = one1[0:1, :]
    sums[7:8, :] = two1[0:1, :]
    sums[8:9, :] = one1[1:2, :]
    sums[9:12, :] = two1[1:4, :]
    for row, qv, u in ((12, qv0, u0), (13, qv1, u1)):
        sums[row : row + 1, :128] = qv[0:1, :]
        sums[row : row + 1, 128:256] = qv[1:2, :]
        sums[row : row + 1, 256:768] = u[...]
    low = sums[...].astype(BF)
    for j, out in enumerate(outs):
        place = lax.rem(at_ref[3] + j, 4)
        for half in range(2):
            rows = pl.ds(pl.multiple_of((half * 4 + place) * 128, 128), 128)
            out[128 * half : 128 * half + 128, :] = full[rows, :]
        out[256:272, :] = low[:, :512]
        out[272:288, :] = low[:, 512:]


def sum_of(refs):
    total = refs[0][...].astype(F32)
    for ref in refs[1:]:
        total = total + ref[...].astype(F32)
    return total


def target_x(at_ref, j):
    x = lax.rem(at_ref[2] * 2 + at_ref[1] + j, 4)
    return lax.rem(x, 2), x // 2


def feed_blocks_body(at_ref, first, second, *outs):
    for j, out in enumerate(outs):
        layer, half = target_x(at_ref, j)
        rows = pl.ds(pl.multiple_of(half * 128, 128), 128)
        out[...] = jnp.where(layer == 0, first[rows, :], second[rows, :])


def attend_blocks_body(at_ref, m0, m1, m2, m3, second, *outs):
    total = sum_of((m0, m1, m2, m3))
    low = total.astype(BF)
    for j, out in enumerate(outs):
        layer, half = target_x(at_ref, j)
        own = jnp.where(half == 0, low[:128], low[128:256])
        rows = pl.ds(pl.multiple_of(half * 128, 128), 128)
        out[:128, :] = jnp.where(layer == 0, own, second[rows, :])
        out[128:, :] = low[256:]


def z_blocks_body(at_ref, a0, a1, a2, a3, f0, f1, f2, f3, o0, o1, o2, o3, rows_ref):
    att = sum_of((a0, a1, a2, a3)).astype(BF)
    rows_ref[:, :512] = att[:128]
    rows_ref[:, 512:] = sum_of((f0, f1, f2, f3)).astype(BF)
    for j, out in enumerate((o0, o1, o2, o3)):
        to = lax.rem(at_ref[0] + j, 4)
        out[:32, :] = rows_ref[pl.ds(pl.multiple_of(to * 32, 32), 32), :]
        out[32:, :512] = att[128:144]
        out[32:, 512:1024] = att[144:160]
        out[32:, 1024:] = jnp.zeros((16, 512), BF)


def finish_body(at_ref, m0, m1, m2, m3, qkv_ref, out_ref, up_ref, down_ref, vector_ref, side_ref):
    row = lax.broadcasted_iota(jnp.int32, (8, 768), 0)
    total = jnp.zeros((16, D), F32)
    side = jnp.zeros((8, 768), F32)
    section = at_ref[1]
    for j, ref in enumerate((m0, m1, m2, m3)):
        place = lax.rem(at_ref[0] + 4 - j, 4)
        narrow = pl.ds(pl.multiple_of(place * 128, 128), 128)
        broad = pl.ds(pl.multiple_of(place * 512, 512), 512)
        for i in range(3):
            qkv_ref[i, :, narrow] = ref[:32, 128 * i : 128 * i + 128].astype(F32)
        out_ref[:, narrow] = ref[:32, 384:512].astype(F32)
        up_ref[:, broad] = ref[:32, 512:1024].astype(F32)
        down_ref[:, broad] = ref[:32, 1024:].astype(F32)
        sums = ref[32:, :1024].astype(F32)
        total = total + sums
        own = jnp.where(section == 0, sums[12:13, :768], sums[13:14, :768])
        side = jnp.where(row == place, own, side)
    vector_ref[...] = jnp.where(section == 0, total[:6], total[6:12])
    index = (at_ref[2] * 4 + at_ref[3]) * 4 + at_ref[0]
    entry = lax.broadcasted_iota(jnp.int32, (8, 768), 1)
    kept = jnp.where(entry % 32 == index, side, 0.0)
    entry = lax.broadcasted_iota(jnp.int32, (768, 128), 0)
    lane = lax.broadcasted_iota(jnp.int32, (768, 128), 1)
    side_ref[...] = dot(kept, (entry // 32 == lane).astype(F32))


def shards(inputs, cotangent, segments, qkv_weight, out_weight, up_weight, down_weight, norm_gains, biases, qv_bias, up_bias):
    section, xh, y, z = (lax.axis_index(name) for name in ("section", "xh", "y", "z"))
    core = lax.axis_index("tensor")
    at = jnp.stack([z, section, xh, y]).astype(jnp.int32)
    x0 = lax.dynamic_index_in_dim(inputs, section, 0, keepdims=False)
    g1 = lax.dynamic_index_in_dim(cotangent, section, 0, keepdims=False)
    own_par = jnp.concatenate([norm_gains[0], biases[0]])
    other_par = swap(own_par, "section")

    sources = (
        qkv_weight[0], out_weight[0].T, up_weight[0], down_weight[0].T, qv_bias[0, :, :, 0], up_bias[0].T
    )
    packed = call(
        pack_body,
        [((112, ATT), BF)] * 4,
        at, *sources,
        scalars=1,
        outside=True,
        vmem=56,
        scratch=[pltpu.VMEM(a.shape, BF) for a in sources] + [pltpu.SemaphoreType.DMA((6,))],
    )
    came = [packed[0]] + [shift(packed[j], "z", -j) for j in (1, 2, 3)]
    att_rows, feed_rows = call(
        collect_body, [((144, ATT), BF), ((128, MLP), BF)], at, *came, scalars=1
    )

    def along_x(part):
        return [part] + [x_shift(part, j) for j in (1, 3, 2)]

    def along_y(layer, pieces, after=()):
        body = lambda *refs: select_body(layer, *refs)
        (rows,) = call(
            body, [((2, *pieces[0].shape), BF)], at, *pieces, scalars=1, after=after
        )
        return [rows] + [shift(rows, "y", j) for j in (1, 2, 3)]

    att_outs = [((D, ATT), BF), ((128, 128), BF)]
    feed_outs = [((D, MLP), BF)]
    att_x = along_x(att_rows)
    att_y = along_y(0, att_x)
    feed_x = along_x(feed_rows)

    row = lax.dynamic_index_in_dim(segments, section, 0, keepdims=False)
    run = lax.dynamic_slice_in_dim(row, (xh * 4 + y) * RUN, RUN)
    marks = jnp.stack([jnp.arange(RUN, dtype=jnp.int32), run]).reshape(2, 4, 2, 64)
    marks = lax.dynamic_slice_in_dim(jnp.concatenate([marks, marks], axis=1), z, 4, 1)
    marks = jnp.where(core == 0, marks, marks[:, :, ::-1])
    marks = jnp.transpose(marks, (0, 2, 1, 3)).reshape(2, RUN)
    allowed = (marks[0][None, :] <= marks[0][:, None]) & (marks[1][None, :] == marks[1][:, None])
    mask = jnp.where(allowed, 0.0, MASKED).astype(F32)

    pars = [
        jnp.where(section == 0, own_par, other_par),
        jnp.where(section == 0, other_par, own_par),
    ]

    half = [((256, D), BF)] * 2
    saved = []
    acts = [None, None]
    weights = []
    rows = x0
    normed = call(first_norm_body, [((128, D), BF)], x0, g1, pars[0])[0]
    for layer in (0, 1):
        par = pars[layer]
        a_rows = gather_rows(normed)
        if layer == 0:
            g_rows = a_rows
            att, side = call(
                place_y_body, att_outs, at, *att_y, scalars=1, after=[*a_rows, mask]
            )
        else:
            att, side = call(
                place_y_body, att_outs, at, *att_y, scalars=1, after=a_rows[:4]
            )
        feed_y = along_y(layer, feed_x, after=(rows,) if layer else (att,))
        *parts, qkv, attended, att_low = call(
            attend_body,
            half + [((3, RUN, 128), BF), ((RUN, 128), F32), ((RUN, 128), BF)],
            *a_rows, att, side, mask, after=(feed_y[0],),
        )
        blocks, added = scatter_rows(*parts)
        hidden, second = call(
            mid_body, [((64, D), F32), ((64, D), BF)], rows, *blocks, par
        )
        b_rows = gather_rows(second)
        (feed,) = call(place_y_body, feed_outs, at, *feed_y, scalars=1, after=b_rows[:4])
        weights.append((att, feed))
        if layer == 0:
            att_y = along_y(1, att_x, after=(feed,))
            *parts, u, gelu_low = call(
                feed_body,
                half + [((RUN, 512), F32), ((RUN, 512), BF)],
                *b_rows, feed, side, after=(att_y[0],),
            )
            blocks, added = scatter_rows(*parts)
            saved.append((rows, a_rows, qkv, attended, att_low, hidden, b_rows, u, gelu_low))
            rows, normed = call(
                end_body, [((64, D), BF)] * 2, hidden, *blocks, par, pars[1]
            )
            acts[0] = rows

    inputs_back = [None, None]
    sums_two = [None, None]
    sums_one = [None, None]
    u_sum = [None, None]
    qv_sum = [None, None]
    feed_sums = [None, None]
    grad_rows = g1

    def halve(messages, after):
        keep, send = messages
        shape = keep.shape[1:]
        mine, later = call(halve_body, [(shape, F32), (shape, BF)], keep, flip(send), after=after)
        return mine, mirror(later)

    def halve_end(pieces, after):
        return call(halve_end_body, [(pieces[0].shape, BF)], *pieces, after=after)[0]

    def message_shapes(n):
        return [((2, 256, n), BF)] * 2

    for layer in (1, 0):
        att, feed = weights[layer]
        par = pars[layer]
        if layer:
            *parts, gelu_low, du, u_sum[1] = call(
                feed_turn_body,
                [((512, D), BF)] * 2 + [((RUN, 512), BF)] * 2 + [((1, 512), F32)],
                *b_rows, *g_rows, feed, side,
            )
            blocks, added = scatter_rows(*parts)
            order = (added,)
        else:
            rows, a_rows, qkv, attended, att_low, hidden, b_rows, u, gelu_low = saved[0]
            g_rows = gather_rows(grad_rows)
            att_step = halve(att_messages, after=())
            *parts, du, u_sum[0] = call(
                feed_back_body, half + [((RUN, 512), BF), ((1, 512), F32)], *g_rows, feed, u,
                after=(feed_sums[1], att_step[0]),
            )
            blocks, added = scatter_rows(*parts)
            grad_att = halve_end(att_step, after=(added,))
            order = (added,)
        body = lambda at_ref, *refs, first=64 * layer: feed_grads(first, at_ref, refs)
        messages = call(
            body, message_shapes(MLP), at, *g_rows, *b_rows, du, gelu_low,
            scalars=1, flops=4 * RUN * D * 512, after=order, scratch=[pltpu.VMEM((D, MLP), BF)],
        )
        if layer:
            acts[1], dh, dh_low, sums_two[1] = call(
                turn_body,
                [((64, D), BF), ((64, D), F32), ((64, D), BF), ((4, D), F32)],
                grad_rows, hidden, *blocks, par, after=(messages[0],),
            )
        else:
            dh, dh_low, sums_two[0] = call(
                mid_back_body,
                [((64, D), F32), ((64, D), BF), ((4, D), F32)],
                grad_rows, hidden, *blocks, par, after=(messages[0],),
            )
        h_rows = gather_rows(dh_low)
        *parts, dqkv, qv_sum[layer] = call(
            attend_back_body,
            half + [((RUN, 384), BF), ((2, 128), F32)],
            *h_rows, att, mask, qkv, attended, after=() if layer else (grad_att,),
        )
        feed_step = halve(messages, after=(dqkv,))
        if layer == 0:
            last = call(
                last_grads_body,
                [((288, ATT), BF)] * 4,
                at, *a_rows, *h_rows, dqkv, att_low, *parts, pars[0],
                sums_two[0], sums_one[1], sums_two[1], qv_sum[0], u_sum[0], qv_sum[1], u_sum[1],
                scalars=1, after=(feed_step[0],), scratch=[pltpu.VMEM((16, D), F32), pltpu.VMEM((D, ATT), BF)],
            )
        blocks, added = scatter_rows(*parts, after=(feed_step[0],) if layer else ())
        feed_sums[layer] = halve_end(feed_step, after=(added,) if layer else (last[0], blocks[1], blocks[2]))
        if layer:
            att_messages = call(
                attend_grads_body, message_shapes(ATT), at, *a_rows, *h_rows, dqkv, att_low,
                scalars=1, flops=2 * RUN * D * 512, after=(added,),
                scratch=[pltpu.VMEM((D, ATT), BF)],
            )
        grad_rows, sums_one[layer] = call(
            end_back_body, [((64, D), BF), ((2, D), F32)], dh, rows, *blocks, par,
            after=(att_messages[0],) if layer else (),
        )
        inputs_back[layer] = grad_rows

    messages = last[:4]
    feed_out = call(
        feed_blocks_body, [((128, MLP), BF)] * 4, at, *feed_sums, scalars=1, after=(messages[0],)
    )
    feed_in = [feed_out[0]] + [x_shift(feed_out[j], -j) for j in (1, 2, 3)]
    att_in = [messages[0]] + [shift(messages[j], "y", -j) for j in (1, 2, 3)]
    att_out = call(
        attend_blocks_body, [((160, ATT), BF)] * 4, at, *att_in, grad_att, scalars=1, after=(feed_in[1],)
    )
    att_in = [att_out[0]] + [x_shift(att_out[j], -j) for j in (1, 2, 3)]
    *out, _ = call(
        z_blocks_body,
        [((48, 1536), BF)] * 4 + [((128, 1536), BF)],
        at, *att_in, *feed_in, scalars=1, after=(grad_rows,),
    )
    came = [out[0]] + [shift(out[j], "z", -j) for j in (1, 2, 3)]
    grad_qkv, grad_out, grad_up, grad_down, vector, side = call(
        finish_body,
        [((3, 32, 512), F32), ((32, 512), F32), ((32, 2048), F32), ((32, 2048), F32), ((6, D), F32), ((8, 128), F32)],
        at, *came, scalars=1,
    )
    vector = vector + swap(vector, "tensor")
    grad_qv = jnp.transpose(side[:4, :8].reshape(4, 2, 4), (1, 0, 2)).reshape(1, 2, 16, 1)
    grad_upb = side[:4, 8:24].reshape(1, 64, 1)

    def own_layer(per_layer):
        kept = jnp.where(section == 0, per_layer[0], per_layer[1])
        sent = swap(jnp.where(section == 0, per_layer[1], per_layer[0]), "section")
        return jnp.stack(
            [jnp.where(section == 0, kept, sent), jnp.where(section == 0, sent, kept)]
        )[None]

    return (
        own_layer(acts),
        own_layer(inputs_back),
        grad_qkv[None],
        grad_out.T[None],
        grad_up[None],
        grad_down.T[None],
        vector[None, 0:2],
        vector[None, 2:6],
        grad_qv,
        grad_upb,
    )


def solution(mesh):
    fine = Mesh(mesh.devices.reshape(2, 2, 4, 4, 2), ("section", "xh", "y", "z", "tensor"))
    dp = ("xh", "y", "z")
    return jax.shard_map(
        shards,
        mesh=fine,
        in_specs=(
            P(None, (*dp, "tensor"), None),
            P(None, (*dp, "tensor"), None),
            P(),
            P("section", None, dp, "tensor"),
            P("section", "tensor", dp),
            P("section", dp, "tensor"),
            P("section", "tensor", dp),
            P("section", None, None),
            P("section", None, None),
            P("section", None, "tensor", dp),
            P("section", "tensor", dp),
        ),
        out_specs=(
            P("section", None, (*dp, "tensor"), None),
            P("section", None, (*dp, "tensor"), None),
            P("section", None, dp, "tensor"),
            P("section", "tensor", dp),
            P("section", dp, "tensor"),
            P("section", "tensor", dp),
            P("section", None, None),
            P("section", None, None),
            P("section", None, "tensor", dp),
            P("section", "tensor", dp),
        ),
        check_vma=False,
    )
```
